256 devices in a mesh: dp: 8 (over x, y_lo), expert: 32 (over z, y_hi, core).
Axes of the slice: x: 4, y: 4 (y_hi: 2, y_lo: 2; y = y_hi * 2 + y_lo), z: 8, core: 2. Of those that a mesh axis runs over, the one named last changes fastest.
Arguments:
- tokens: bfloat16 [32768, 2048], P(('dp', 'expert')), may hold values from -6 to 6
- routes: int32 [32768, 2], P(('dp', 'expert')), may hold values from 0 to 31, all different within a row; in each aligned block of 128 rows (0 to 127, 128 to 255, ...) at most 16 rows name the same one
- gate_probs: bfloat16 [32768, 2], P(('dp', 'expert')), may hold values from 0.049804688 to 1
- cotangent: bfloat16 [32768, 2048], P(('dp', 'expert')), may hold values from -6 to 6
- expert_weights: bfloat16 [32, 2048, 2304], P('expert'), may hold values from -0.125 to 0.125
Outputs:
- token_grads: bfloat16 [32768, 2048], P(('dp', 'expert'))
- prob_grads: float32 [32768, 2], P(('dp', 'expert'))
- weight_grads: float32 [32, 2048, 2304], P('expert', 'dp')
The draws below stay inside these ranges and needn't reach their ends.
Inputs may be any that keep to these rules, and one draw needn't show every extreme that they name: `routes`: each token names 2 different experts and every expert is named by some token. In each aligned block of 128 tokens (the tokens of one device) no expert is named by more than 16 tokens, and in some block one expert is named by exactly 16.
All inputs are finite; a program needn't handle non-finite values.
Results may differ from the reference program's by a relative error of at most 0.017.
Values may be sent and summed in bfloat16 or wider, within the bound.
No kernel may reach another device: no remote copies, remote signals or barrier semaphores. Data moves between devices by JAX's collectives and lax.ppermute only.
A program may use at most 192 MiB of HBM per device.

```python
import math
import jax
import jax.numpy as jnp
import numpy as np
from jax import lax

D = 2048
F = 768
TOPK = 2
TOK_DEV = 128
EXPERTS = 32
CAP = 16
TOKENS = 32768
N_DP = 8
N_EXPERT = 32


def levels(rng, extent, shards, low, largest):
    gain = 1.0
    for position, shards_of in shards:
        draws = jax.random.uniform(jax.random.fold_in(jax.random.fold_in(rng, 6), position), (shards_of,), jnp.float32, low / len(shards), largest / len(shards))
        gain = gain * jnp.repeat(jnp.exp(draws), extent[position] // shards_of).reshape((-1,) + (1,) * (len(extent) - 1 - position))
    return gain


def deal_out(rng, own, number, rows, amount, top, limit, slope):
    ranking = jax.random.permutation(rng, amount)
    packed, ordinary = portions_of(amount, rows * top, limit, slope, True), portions_of(amount, rows * top, limit, slope, False)
    places = jnp.arange(amount)

    def named(tallies, rotation):
        used = int((tallies > 0).sum())
        fixed = max(1, used // 4)
        shifted = fixed + (places - fixed + rotation * (used - fixed)) % max(1, amount - fixed)
        return jnp.zeros((amount,), jnp.int32).at[ranking[jnp.where(places < fixed, places, shifted)]].set(jnp.asarray(tallies, jnp.int32))

    tallies = jnp.where(number % 4 == 0, named(packed, number // 4), named(ordinary, number - number // 4 - 1))
    mixed = jax.random.permutation(jax.random.fold_in(own, 3), amount)
    giver, sink = mixed[0:amount // 2 * 2:2], mixed[1:amount // 2 * 2:2]
    slack = jnp.minimum(tallies[giver] - 1, limit - tallies[sink]) // 2
    slack = jnp.where((giver == ranking[0]) | (sink == ranking[0]) | (tallies[sink] == 0), 0, jnp.maximum(slack, 0))
    shifted = jax.random.randint(jax.random.fold_in(own, 4), (amount // 2,), 0, 1 << 20) % (slack + 1)
    tallies = tallies.at[giver].add(-shifted).at[sink].add(shifted)
    labels = jnp.searchsorted(jnp.cumsum(tallies), jnp.arange(rows * top), side="right").astype(jnp.int32)
    listing = labels.reshape(top, rows).T
    listing = listing[jax.random.permutation(jax.random.fold_in(own, 1), rows)]
    rotation = jax.random.randint(jax.random.fold_in(own, 2), (rows, 1), 0, top)
    return jnp.take_along_axis(listing, (jnp.arange(top)[None, :] + rotation) % top, axis=1)


def portions_of(amount, total, reach, slope, full):
    weights = [(1 << 20) // math.isqrt(rank ** slope) + 1 for rank in range(1, amount + 1)]
    largest = reach if full else min(reach, max(-(-total // amount), total * weights[0] // sum(weights)))
    least = 1 if total - largest >= amount - 1 else 0
    holding, spare = [largest] + [least] * (amount - 1), total - largest - least * (amount - 1)
    while spare > 0:
        candidates = [i for i in range(1, amount) if holding[i] < largest] or [i for i in range(1, amount) if holding[i] < reach]
        whole, remaining = sum([weights[i] for i in candidates]), spare
        for i in candidates:
            extra = min(reach - holding[i], max(1, remaining * weights[i] // whole), spare)
            holding[i] = holding[i] + extra
            spare = spare - extra
    return np.array(holding)


def noise(own_key, dims, spread, reach, cuts=(), held_as=jnp.bfloat16):
    values = jax.random.normal(own_key, dims, jnp.float32) * spread
    if len(cuts) > 0:
        values = levels(own_key, dims, cuts, -0.22, 0.18) * values
    return jnp.clip(values, min=-reach, max=reach).astype(held_as)


def setup_inputs(seed: int = 0) -> dict:
    arg_keys = jax.random.split(jax.random.key(seed), 6)
    tokens = noise(arg_keys[0], (TOKENS, D), 1.0, 6.0, ((0, 256),))
    routes_keys = jax.random.split(jax.random.fold_in(arg_keys[1], 1), TOKENS // TOK_DEV)
    routes_turns = jax.random.permutation(jax.random.fold_in(arg_keys[1], 3), TOKENS // TOK_DEV)
    routes = jax.vmap(lambda own, number: deal_out(jax.random.fold_in(arg_keys[1], 2), own, number, TOK_DEV, EXPERTS, TOPK, CAP, 2))(routes_keys, routes_turns).reshape((TOKENS, TOPK))
    gate_probs = jnp.clip(0.049804688 + 0.9501953 * jax.random.uniform(arg_keys[2], (TOKENS, TOPK), jnp.float32) ** levels(arg_keys[2], (TOKENS, TOPK), ((0, 256),), -0.2, 0.2), 0.049804688, 1.0).astype(jnp.bfloat16)
    cotangent = noise(arg_keys[3], (TOKENS, D), 1.0, 6.0, ((0, 256),))
    expert_weights = noise(arg_keys[4], (EXPERTS, D, 3 * F), D ** -0.5, 0.125, ((0, 32),))
    return {"tokens": tokens, "routes": routes, "gate_probs": gate_probs, "cotangent": cotangent, "expert_weights": expert_weights}


def expert_pass(input_rows, grad_rows, prob_rows, matrices):
    hidden_units = matrices.shape[1] // 3
    gate_up = jnp.dot(input_rows, matrices[:, :2 * hidden_units], preferred_element_type=jnp.float32)
    gate_pre = gate_up[:, :hidden_units]
    upward = gate_up[:, hidden_units:]
    sigmoid_gate = jax.nn.sigmoid(gate_pre)
    active = gate_pre * sigmoid_gate
    hidden_act = (active * upward).astype(jnp.bfloat16)
    down_cols = matrices[:, 2 * hidden_units:]
    expert_out = jnp.dot(hidden_act, down_cols.T, preferred_element_type=jnp.float32).astype(jnp.bfloat16)
    scaled = (prob_rows.astype(jnp.float32)[:, None] * grad_rows.astype(jnp.float32)).astype(jnp.bfloat16)
    grad_hidden = jnp.dot(scaled, down_cols, preferred_element_type=jnp.float32)
    grad_gate = (grad_hidden * upward * sigmoid_gate * (1.0 + gate_pre * (1.0 - sigmoid_gate))).astype(jnp.bfloat16)
    grad_up = (grad_hidden * active).astype(jnp.bfloat16)
    factors = jnp.concatenate([grad_gate, grad_up, hidden_act], axis=1)
    grad_input = jnp.dot(factors[:, :2 * hidden_units], matrices[:, :2 * hidden_units].T,
                         preferred_element_type=jnp.float32).astype(jnp.bfloat16)
    return expert_out, grad_input, factors, scaled


def reference(tokens, routes, gate_probs, cotangent, expert_weights):
    token_total, features = tokens.shape
    chosen = routes.shape[1]
    pair_count = token_total * chosen
    flat_routes = routes.reshape(pair_count)
    bound_rows = N_DP * N_EXPERT * CAP
    hidden_units = expert_weights.shape[2] // 3
    zero_row = jnp.zeros((1, features), jnp.bfloat16)
    token_pad = jnp.concatenate([tokens, zero_row], axis=0)
    grad_pad = jnp.concatenate([cotangent, zero_row], axis=0)
    prob_pad = jnp.concatenate([gate_probs.reshape(pair_count), jnp.zeros((1,), jnp.bfloat16)])

    def one_expert(carry, expert):
        token_acc, prob_acc = carry
        picked = jnp.nonzero(flat_routes == expert, size=bound_rows, fill_value=pair_count)[0].astype(jnp.int32)
        owners = (picked // chosen).astype(jnp.int32)
        input_rows = token_pad[owners]
        grad_rows = grad_pad[owners]
        prob_rows = prob_pad[picked]
        matrices = expert_weights[expert]
        expert_out, grad_input, factors, scaled = expert_pass(input_rows, grad_rows, prob_rows, matrices)
        first = jnp.dot(input_rows.T, factors[:, :2 * hidden_units], preferred_element_type=jnp.float32)
        second = jnp.dot(scaled.T, factors[:, 2 * hidden_units:], preferred_element_type=jnp.float32)
        grads = jnp.concatenate([first, second], axis=1)
        token_acc = token_acc.at[owners].add(grad_input.astype(jnp.float32), mode="drop")
        products = jnp.sum(grad_rows.astype(jnp.float32) * expert_out.astype(jnp.float32), axis=1)
        prob_acc = prob_acc.at[picked].add(products, mode="drop")
        return (token_acc, prob_acc), grads

    initial = (jnp.zeros((token_total, features), jnp.float32), jnp.zeros((pair_count,), jnp.float32))
    (token_acc, prob_acc), weight_grads = lax.scan(one_expert, initial, jnp.arange(EXPERTS, dtype=jnp.int32))
    return token_acc.astype(jnp.bfloat16), prob_acc.reshape(token_total, chosen), weight_grads
```

```python
import functools

import jax
import jax.numpy as jnp
from jax import lax
from jax.experimental import pallas as pl
from jax.experimental.pallas import tpu as pltpu
from jax.sharding import PartitionSpec as P

BF = jnp.bfloat16
F32 = jnp.float32
D = 2048
F = 768
T = 128
CAP = 16
NZ = 8
NQ = 4
FB = 256


def z_shift(value, step):
    return lax.ppermute(value, "expert", [(i, (i + NQ * step) % 32) for i in range(32)])


def plane_swap(value, mask):
    return lax.ppermute(value, "expert", [(i, i ^ mask) for i in range(32)])


def x_shift(value, step):
    return lax.ppermute(value, "dp", [(i, (i + 2 * step) % 8) for i in range(8)])


def y_swap(value):
    return lax.ppermute(value, "dp", [(i, i ^ 1) for i in range(8)])


def slots(route_pairs, experts):
    first = route_pairs[:, 0][:, None, :] == experts[None, :, None]
    second = route_pairs[:, 1][:, None, :] == experts[None, :, None]
    named = first | second
    before = (jnp.arange(T)[:, None] < jnp.arange(T)[None, :]).astype(BF)
    position = jnp.einsum("bet,tu->beu", named.astype(BF), before, preferred_element_type=F32)
    place = jnp.arange(CAP, dtype=F32)[None, None, :, None]
    hot = named[:, :, None, :] & (position[:, :, None, :] == place)
    return hot, first, second


def select_kernel(blocks, hot_ref, *refs):
    ins, outs = refs[:blocks], refs[blocks:]
    for i in range(blocks):
        rows = jnp.dot(hot_ref[0, i], ins[i][...], preferred_element_type=F32).astype(BF)
        for j in range(NQ):
            outs[j][i * CAP : (i + 1) * CAP, :] = rows[j * CAP : (j + 1) * CAP, :]


def select(hot, ins):
    n = len(ins)
    width = 1024
    return pl.pallas_call(
        functools.partial(select_kernel, n),
        grid=(2 * D // width,),
        in_specs=[pl.BlockSpec((1, n, NQ * CAP, T), lambda c: (c // 2, 0, 0, 0))]
        + [pl.BlockSpec((T, width), lambda c: (0, c))] * n,
        out_specs=[pl.BlockSpec((n * CAP, width), lambda c: (0, c))] * NQ,
        out_shape=[jax.ShapeDtypeStruct((n * CAP, 2 * D), BF)] * NQ,
        cost_estimate=pl.CostEstimate(
            flops=2 * n * 64 * T * 2 * D, bytes_accessed=n * 3 * T * D * 2, transcendentals=0
        ),
        compiler_params=pltpu.CompilerParams(vmem_limit_bytes=24 * 1024 * 1024),
    )(hot, *ins)


def expert_kernel(part, gate_w, up_w, down_w, a, b, c, d, xs, fac, grad_in, dots, acc, dot_acc):
    f = pl.program_id(0)

    @pl.when(f == 0)
    def _():
        for j, ref in enumerate((a, b, c, d)):
            xs[j * part : (j + 1) * part, :] = ref[...]
        acc[...] = jnp.zeros_like(acc)
        dot_acc[...] = jnp.zeros_like(dot_acc)

    x = xs[:, :D]
    gate = jnp.dot(x, gate_w[...], preferred_element_type=F32)
    up = jnp.dot(x, up_w[...], preferred_element_type=F32)
    dh = jnp.dot(xs[:, D:], down_w[...], preferred_element_type=F32)
    sig = jax.nn.sigmoid(gate)
    active = gate * sig
    hidden = (active * up).astype(BF)
    d_gate = (dh * up * sig * (1.0 + gate * (1.0 - sig))).astype(BF)
    d_up = (dh * active).astype(BF)
    at = pl.multiple_of(f * FB, FB)
    fac[:, pl.ds(at, FB)] = d_gate
    fac[:, pl.ds(F + at, FB)] = d_up
    fac[:, pl.ds(2 * F + at, FB)] = hidden
    nt = (((1,), (1,)), ((), ()))
    acc[...] += lax.dot_general(d_gate, gate_w[...], nt, preferred_element_type=F32)
    acc[...] += lax.dot_general(d_up, up_w[...], nt, preferred_element_type=F32)
    prod = hidden.astype(F32) * dh
    dot_acc[...] += prod[:, :128] + prod[:, 128:]

    @pl.when(f == F // FB - 1)
    def _():
        grad_in[...] = acc[...].astype(BF)
        dots[...] = jnp.broadcast_to(jnp.sum(dot_acc[...], axis=1, keepdims=True), dots.shape)


def expert_pass(weights, pieces):
    part = pieces[0].shape[0]
    rows = NQ * part
    whole = lambda f: (0, 0)
    return pl.pallas_call(
        functools.partial(expert_kernel, part),
        grid=(F // FB,),
        in_specs=[
            pl.BlockSpec((D, FB), lambda f: (0, f)),
            pl.BlockSpec((D, FB), lambda f: (0, f + F // FB)),
            pl.BlockSpec((D, FB), lambda f: (0, f + 2 * F // FB)),
        ]
        + [pl.BlockSpec((part, 2 * D), whole)] * NQ,
        out_specs=[
            pl.BlockSpec((rows, 2 * D), whole),
            pl.BlockSpec((rows, 3 * F), whole),
            pl.BlockSpec((rows, D), whole),
            pl.BlockSpec((rows, 128), whole),
        ],
        out_shape=[
            jax.ShapeDtypeStruct((rows, 2 * D), BF),
            jax.ShapeDtypeStruct((rows, 3 * F), BF),
            jax.ShapeDtypeStruct((rows, D), BF),
            jax.ShapeDtypeStruct((rows, 128), F32),
        ],
        scratch_shapes=[pltpu.VMEM((rows, D), F32), pltpu.VMEM((rows, 128), F32)],
        cost_estimate=pl.CostEstimate(
            flops=2 * rows * D * 5 * F, bytes_accessed=D * 3 * F * 2, transcendentals=rows * F
        ),
        compiler_params=pltpu.CompilerParams(vmem_limit_bytes=32 * 1024 * 1024),
    )(weights, weights, weights, *pieces)


def to_expert(weights, hot, ins):
    own, one, two, three = select(hot, ins)
    return expert_pass(
        weights, [own, plane_swap(one, 1), plane_swap(two, 2), plane_swap(three, 3)]
    )


def weight_grads_of(xs, fac):
    dp = lax.axis_index("dp")
    xi, yi = dp // 2, dp % 2
    dims = (((0,), (0,)), ((), ()))

    def left(offset, chunk, half, start=0, size=256):
        at = offset + ((xi + chunk) % 4) * 512 + half * 256 + start
        return lax.dynamic_slice(xs, (0, at), (xs.shape[0], size))

    def product(l, r):
        return lax.dot_general(l, r, dims, preferred_element_type=F32)

    ab = fac[:, : 2 * F]
    hid = fac[:, 2 * F :]

    def first(chunk, half):
        return product(left(0, chunk, half), ab)

    far_r = x_shift(first(2, 0).astype(BF), 1)
    far_l = x_shift(first(2, 1).astype(BF), -1)
    others = lax.dynamic_index_in_dim(xs[:, D:].reshape(-1, 4, 2, 256), 1 - yi, 2, False)
    from_y = y_swap(product(others.reshape(-1, 1024), hid).astype(BF))
    near_r = x_shift(first(1, 1).astype(BF), 1)
    near_l = x_shift(first(-1, 0).astype(BF), -1)
    last_r = x_shift((first(1, 0) + far_r.astype(F32)).astype(BF), 1)
    last_l = x_shift((first(-1, 1) + far_l.astype(F32)).astype(BF), -1)

    def second(chunk, start):
        arrived = lax.dynamic_slice(from_y, (((xi + chunk) % 4) * 256 + start, 0), (128, F))
        return product(left(D, chunk, yi, start, 128), hid) + arrived.astype(F32)

    sfar_r = x_shift(second(2, 0).astype(BF), 1)
    sfar_l = x_shift(second(2, 128).astype(BF), -1)
    snear_r = x_shift(second(1, 128).astype(BF), 1)
    snear_l = x_shift(second(-1, 0).astype(BF), -1)
    slast_r = x_shift((second(1, 0) + sfar_r.astype(F32)).astype(BF), 1)
    slast_l = x_shift((second(-1, 128) + sfar_l.astype(F32)).astype(BF), -1)

    zero = yi == 0
    sum0 = near_l.astype(F32) + last_r.astype(F32)
    sum1 = near_r.astype(F32) + last_l.astype(F32)
    away = (first(0, 1 - yi) + jnp.where(zero, sum1, sum0)).astype(BF)
    mine = first(0, yi) + jnp.where(zero, sum0, sum1)
    done_ab = mine + y_swap(away).astype(F32)
    s0 = second(0, 0) + snear_l.astype(F32) + slast_r.astype(F32)
    s1 = second(0, 128) + snear_r.astype(F32) + slast_l.astype(F32)
    return jnp.concatenate([done_ab, jnp.concatenate([s0, s1], axis=0)], axis=1)


def shards(tokens, routes, gate_probs, cotangent, expert_weights):
    me = lax.axis_index("expert")
    z, q = me // NQ, me % NQ
    weights = expert_weights[0]

    home = jnp.concatenate([tokens, cotangent], axis=1)
    ahead, behind = [home], [home]
    for _ in range(3):
        ahead.append(z_shift(ahead[-1], 1))
        behind.append(z_shift(behind[-1], -1))
    opposite = jnp.concatenate(
        [z_shift(ahead[3][: T // 2], 1), z_shift(behind[3][T // 2 :], -1)], axis=0
    )

    meta = jnp.concatenate([routes.T.astype(BF), gate_probs.T], axis=0)
    groups = [[p * NQ + i for p in range(NZ)] for i in range(NQ)]
    metas = lax.all_to_all(
        jnp.broadcast_to(meta[None], (NZ, 4, T)),
        "expert",
        split_axis=0,
        concat_axis=0,
        tiled=True,
        axis_index_groups=groups,
    )
    metas = lax.dynamic_slice(jnp.concatenate([metas, metas], axis=0), (z, 0, 0), (NZ, 4, T))
    near = jnp.arange(NQ, dtype=jnp.int32)
    plane = (z * NQ + jnp.bitwise_xor(q, near)).astype(F32)
    hot, first, second = slots(metas[:, :2].astype(F32), plane)
    p0 = metas[:, 2][:, None, :].astype(F32)
    p1 = metas[:, 3][:, None, :].astype(F32)
    weight = jnp.where(first, p0, 0.0) + jnp.where(second, p1, 0.0)
    weighted = jnp.where(hot, weight[:, :, None, :], 0.0).astype(BF)
    both = jnp.stack([hot.astype(BF), weighted]).reshape(2, NZ, NQ * CAP, T)

    def hot_of(distances):
        return jnp.stack([both[:, d % NZ] for d in distances], axis=1)

    steps = [
        ((0,), [home]),
        ((-1, 1), [ahead[1], behind[1]]),
        ((-2, 2), [ahead[2], behind[2]]),
        ((-3, 3), [ahead[3], behind[3]]),
        ((4,), [opposite]),
    ]
    results = [to_expert(weights, hot_of(ds), ins) for ds, ins in steps]
    xs = jnp.concatenate([r[0] for r in results], axis=0)
    fac = jnp.concatenate([r[1] for r in results], axis=0)
    weight_grads = weight_grads_of(xs, fac)

    order = [(d % NZ, j, ) for ds, _ in steps for j in range(NQ) for d in ds]
    where = {pair: i for i, pair in enumerate(order)}
    table = jnp.array([[where[(d, j)] for j in range(NQ)] for d in range(NZ)], jnp.int32)
    target = jnp.arange(NZ * NQ, dtype=jnp.int32)
    index = table[(target // NQ - z) % NZ, jnp.bitwise_xor(target % NQ, q)]
    grad_rows = jnp.concatenate([r[2] for r in results], axis=0).reshape(32, CAP, D)
    dot_rows = jnp.concatenate([r[3][:, 0] for r in results], axis=0).reshape(32, CAP)
    back = lax.all_to_all(
        jnp.take(grad_rows, index, axis=0), "expert", split_axis=0, concat_axis=0, tiled=True
    ).reshape(32 * CAP, D)
    dots = lax.all_to_all(
        jnp.take(dot_rows, index, axis=0), "expert", split_axis=0, concat_axis=0, tiled=True
    )

    hot_home, one, two = slots(routes.T[None].astype(F32), jnp.arange(32, dtype=F32))
    hot_home = hot_home[0]
    token_grads = lax.dot_general(
        hot_home.reshape(32 * CAP, T).astype(BF),
        back,
        (((0,), (0,)), ((), ())),
        preferred_element_type=F32,
    ).astype(BF)
    found = jnp.sum(jnp.where(hot_home, dots[:, :, None], 0.0), axis=1)
    prob = jnp.stack(
        [
            jnp.sum(jnp.where(one[0], found, 0.0), axis=0),
            jnp.sum(jnp.where(two[0], found, 0.0), axis=0),
        ],
        axis=1,
    )
    prob_grads = prob / gate_probs.astype(F32)
    return token_grads, prob_grads, weight_grads[None]


def solution(mesh):
    rows = P(("dp", "expert"), None)
    return jax.shard_map(
        shards,
        mesh=mesh,
        in_specs=(rows, rows, rows, rows, P("expert", None, None)),
        out_specs=(rows, rows, P("expert", "dp", None)),
        check_vma=False,
    )
```

```python
import functools

import jax
import jax.numpy as jnp
from jax import lax
from jax.experimental import pallas as pl
from jax.experimental.pallas import tpu as pltpu
from jax.sharding import PartitionSpec as P

BF = jnp.bfloat16
F32 = jnp.float32
I32 = jnp.int32
D = 2048
F = 768
T = 128
CAP = 16
NZ = 8
NQ = 4
FB = 256
NF = F // FB
ROWS = NZ * NQ * CAP
EXTRA = 128
MIB = 1024 * 1024
NT = (((1,), (1,)), ((), ()))
TN = (((0,), (0,)), ((), ()))
ANY = pl.BlockSpec(memory_space=pl.ANY)
together = lax.optimization_barrier


def z_shift(value, step):
    return lax.ppermute(value, "expert", [(i, (i + NQ * step) % 32) for i in range(32)])


def plane_swap(value, mask):
    return lax.ppermute(value, "expert", [(i, i ^ mask) for i in range(32)])


def diagonal(value, step, mask):
    return lax.ppermute(value, "expert", [(i, ((i ^ mask) + NQ * step) % 32) for i in range(32)])


def x_shift(value, step):
    return lax.ppermute(value, "dp", [(i, (i + 2 * step) % 8) for i in range(8)])


def y_swap(value):
    return lax.ppermute(value, "dp", [(i, i ^ 1) for i in range(8)])


def params(mib):
    return pltpu.CompilerParams(vmem_limit_bytes=mib * MIB)


def cost(flops, moved):
    return pl.CostEstimate(flops=flops // 1024, bytes_accessed=moved // 1024, transcendentals=0)


def columns(pairs):
    diagonal = lax.broadcasted_iota(I32, (T, T), 0) == lax.broadcasted_iota(I32, (T, T), 1)
    eye = diagonal.astype(F32).astype(BF)
    return lax.dot_general(eye, pairs.astype(F32).astype(BF), NT, preferred_element_type=F32)


def pack_kernel(tokens, cotangent, routes, probs, out):
    out[:, :D] = tokens[...]
    out[:, D : 2 * D] = cotangent[...]
    lane = lax.broadcasted_iota(I32, (T, EXTRA), 1)
    r, p = columns(routes[...]), columns(probs[...])
    meta = jnp.where(lane == 0, r[:, 0:1], jnp.where(lane == 1, r[:, 1:2], 0.0))
    meta += jnp.where(lane == 2, p[:, 0:1], jnp.where(lane == 3, p[:, 1:2], 0.0))
    out[:, 2 * D :] = meta.astype(BF)


def pack(tokens, cotangent, routes, probs):
    return pl.pallas_call(
        pack_kernel,
        out_shape=jax.ShapeDtypeStruct((T, 2 * D + EXTRA), BF),
        cost_estimate=cost(0, 4 * T * D * 2),
        compiler_params=params(8),
    )(tokens, cotangent, routes.T, probs.T)


def slots(r0, r1, expert, place):
    first = (r0 == expert).astype(F32)
    second = (r1 == expert).astype(F32)
    named = first + second
    row = lax.broadcasted_iota(I32, (T, T), 0)
    col = lax.broadcasted_iota(I32, (T, T), 1)
    before = (col < row).astype(F32).astype(BF)
    position = jnp.dot(before, named.astype(BF), preferred_element_type=F32)
    here = (position == place).astype(F32)
    return first * here, second * here


def select_kernel(plan, split, *refs):
    n = len(plan)
    metas, ins, outs, hot = refs[:n], refs[n : 2 * n], refs[2 * n : -1], refs[-1]
    c = pl.program_id(0)

    @pl.when(c == 0)
    def _():
        me = lax.axis_index("expert")
        z, q = me // NQ, me % NQ
        for i, (step, begin, end) in enumerate(plan):
            lane = lax.broadcasted_iota(I32, (T, NQ * CAP), 1)
            plane = (z + step + NZ) % NZ
            expert = (plane * NQ + jnp.bitwise_xor(q, lane // CAP)).astype(F32)
            place = (lane % CAP).astype(F32)
            meta = metas[i][...].astype(F32)
            one, two = slots(meta[:, 0:1], meta[:, 1:2], expert, place)
            hot[0, i] = (one + two).astype(BF)
            hot[1, i] = (one * meta[:, 2:3] + two * meta[:, 3:4]).astype(BF)

    for i, (_, begin, end) in enumerate(plan):
        mat = hot[c // 2, i]
        rows = lax.dot_general(mat, ins[i][...], TN, preferred_element_type=F32).astype(BF)
        if split:
            for j in range(NQ):
                outs[j][i * CAP : (i + 1) * CAP, :] = rows[j * CAP : (j + 1) * CAP, :]
        else:
            for j in range(begin, end):
                outs[2 * i + j - begin][...] = rows[j * CAP : (j + 1) * CAP, :]


def select(plan, ins, split):
    n = len(ins)
    width = 1024
    count, height = (NQ, n * CAP) if split else (2 * n, CAP)
    return pl.pallas_call(
        functools.partial(select_kernel, plan, split),
        grid=(2 * D // width,),
        in_specs=[pl.BlockSpec((T, EXTRA), lambda c: (0, 2 * D // EXTRA))] * n
        + [pl.BlockSpec((T, width), lambda c: (0, c))] * n,
        out_specs=[pl.BlockSpec((height, width), lambda c: (0, c))] * count,
        out_shape=[jax.ShapeDtypeStruct((height, 2 * D), BF)] * count,
        scratch_shapes=[pltpu.VMEM((2, n, T, NQ * CAP), BF)],
        cost_estimate=cost(2 * n * 64 * T * 2 * D, n * 3 * T * D * 2),
        compiler_params=params(10),
    )(*ins, *ins)


def dot_columns(dots):
    lane = lax.broadcasted_iota(I32, dots.shape, 1)
    high = dots.astype(BF).astype(F32)
    return jnp.where(lane == 0, high, jnp.where(lane == 1, dots - high, 0.0)).astype(BF)


def place_rows(order, out_rows, grad_all, sems):
    me = lax.axis_index("expert")
    z, q = me // NQ, me % NQ
    copies = []
    for i, (step, near) in enumerate(order):
        owner = ((z + step + NZ) % NZ) * NQ + jnp.bitwise_xor(q, near)
        copies.append(
            pltpu.make_async_copy(
                out_rows.at[pl.ds(i * CAP, CAP)],
                grad_all.at[pl.ds(pl.multiple_of(owner * CAP, CAP), CAP)],
                sems.at[i],
            )
        )
    for copy in copies:
        copy.start()
    for copy in copies:
        copy.wait()


def expert_kernel(pieces, order, grads, aliased, gate_w, up_w, down_w, *refs):
    ins = refs[: len(pieces)]
    refs = refs[len(pieces) + aliased :]
    if grads:
        xs, fac, grad_all, rows, dot_acc, acc, out_rows, sems = refs
    else:
        xs, fac, dots, rows, dot_acc = refs
    f = pl.program_id(0)

    @pl.when(f == 0)
    def _():
        at = 0
        for size, ref in zip(pieces, ins):
            rows[at : at + size, :] = ref[...]
            at += size
        dot_acc[...] = jnp.zeros_like(dot_acc)
        if grads:
            acc[...] = jnp.zeros_like(acc)

    x = rows[:, :D]
    gate = jnp.dot(x, gate_w[...], preferred_element_type=F32)
    up = jnp.dot(x, up_w[...], preferred_element_type=F32)
    dh = jnp.dot(rows[:, D:], down_w[...], preferred_element_type=F32)
    sig = jax.nn.sigmoid(gate)
    active = gate * sig
    hidden = (active * up).astype(BF)
    d_gate = (dh * up * sig * (1.0 + gate * (1.0 - sig))).astype(BF)
    d_up = (dh * active).astype(BF)
    at = pl.multiple_of(f * FB, FB)
    fac[:, pl.ds(at, FB)] = d_gate
    fac[:, pl.ds(F + at, FB)] = d_up
    fac[:, pl.ds(2 * F + at, FB)] = hidden
    prod = hidden.astype(F32) * dh
    dot_acc[...] += prod[:, :128] + prod[:, 128:]
    if grads:
        acc[...] += lax.dot_general(d_gate, gate_w[...], NT, preferred_element_type=F32)
        acc[...] += lax.dot_general(d_up, up_w[...], NT, preferred_element_type=F32)

    @pl.when(f == NF - 1)
    def _():
        dp = lax.axis_index("dp")
        xi, yi = dp // 2, dp % 2
        for part in range(2):
            for chunk in range(4):
                for half in range(2):
                    source = ((xi + chunk) % 4) * 2 + jnp.bitwise_xor(yi, half)
                    source = pl.multiple_of(part * D + source * 256, 256)
                    to = part * D + (chunk * 2 + half) * 256
                    xs[:, to : to + 256] = rows[:, pl.ds(source, 256)]
        total = jnp.sum(dot_acc[...], axis=1, keepdims=True)
        total = jnp.broadcast_to(total, dot_acc.shape)
        if grads:
            out_rows[:, :D] = acc[...].astype(BF)
            out_rows[:, D:] = dot_columns(total)
            place_rows(order, out_rows, grad_all, sems)
        else:
            dots[...] = total


def expert_pass(weights, pieces, order, block, held, grads):
    sizes = [piece.shape[0] for piece in pieces]
    rows = sum(sizes)
    whole = lambda f: (0, 0)
    mine = lambda f: (block, 0)
    outs = [pl.BlockSpec((rows, 2 * D), mine), pl.BlockSpec((rows, 3 * F), mine)]
    shapes = [jax.ShapeDtypeStruct((ROWS, 2 * D), BF), jax.ShapeDtypeStruct((ROWS, 3 * F), BF)]
    scratch = [pltpu.VMEM((rows, 2 * D), BF), pltpu.VMEM((rows, 128), F32)]
    if grads:
        outs.append(ANY)
        shapes.append(jax.ShapeDtypeStruct((ROWS, D + EXTRA), BF))
        scratch += [
            pltpu.VMEM((rows, D), F32),
            pltpu.VMEM((rows, D + EXTRA), BF),
            pltpu.SemaphoreType.DMA((rows // CAP,)),
        ]
    else:
        outs.append(pl.BlockSpec((rows, 128), whole))
        shapes.append(jax.ShapeDtypeStruct((rows, 128), F32))
    return pl.pallas_call(
        functools.partial(expert_kernel, sizes, order, grads, len(held)),
        grid=(NF,),
        in_specs=[
            pl.BlockSpec((D, FB), lambda f: (0, f)),
            pl.BlockSpec((D, FB), lambda f: (0, f + NF)),
            pl.BlockSpec((D, FB), lambda f: (0, f + 2 * NF)),
        ]
        + [pl.BlockSpec((size, 2 * D), whole) for size in sizes]
        + [ANY] * len(held),
        out_specs=outs,
        out_shape=shapes,
        scratch_shapes=scratch,
        input_output_aliases={3 + len(pieces) + i: i for i in range(len(held))},
        cost_estimate=cost(2 * rows * D * (5 if grads else 3) * F, D * 3 * F * 2),
        compiler_params=params(24),
    )(weights, weights, weights, *pieces, *held)


def grad_kernel(order, gate_w, up_w, gate_f, up_f, dots, held, grad_all, acc, out_rows, sems):
    f = pl.program_id(0)

    @pl.when(f == 0)
    def _():
        acc[...] = jnp.zeros_like(acc)

    acc[...] += lax.dot_general(gate_f[...], gate_w[...], NT, preferred_element_type=F32)
    acc[...] += lax.dot_general(up_f[...], up_w[...], NT, preferred_element_type=F32)

    @pl.when(f == NF - 1)
    def _():
        out_rows[:, :D] = acc[...].astype(BF)
        out_rows[:, D:] = dot_columns(dots[...])
        place_rows(order, out_rows, grad_all, sems)


def grad_pass(weights, fac, block, dots, order, grad_all):
    rows = dots.shape[0]
    return pl.pallas_call(
        functools.partial(grad_kernel, order),
        grid=(NF,),
        in_specs=[
            pl.BlockSpec((D, FB), lambda f: (0, f)),
            pl.BlockSpec((D, FB), lambda f: (0, f + NF)),
            pl.BlockSpec((rows, FB), lambda f: (block, f)),
            pl.BlockSpec((rows, FB), lambda f: (block, f + NF)),
            pl.BlockSpec((rows, 128), lambda f: (0, 0)),
            ANY,
        ],
        out_specs=ANY,
        out_shape=jax.ShapeDtypeStruct(grad_all.shape, BF),
        scratch_shapes=[
            pltpu.VMEM((rows, D), F32),
            pltpu.VMEM((rows, D + EXTRA), BF),
            pltpu.SemaphoreType.DMA((rows // CAP,)),
        ],
        input_output_aliases={5: 0},
        cost_estimate=cost(4 * rows * D * F, D * 2 * F * 2),
        compiler_params=params(20),
    )(weights, weights, fac, fac, dots, grad_all)


def parts_kernel(n, *refs):
    fac = refs[n][...]
    for i in range(n):
        out = refs[n + 1 + i]
        total = lax.dot_general(refs[i][...], fac, TN, preferred_element_type=F32)
        out[...] = total.astype(out.dtype)


def parts(xs, fac, plan, dtype, stacked=False):
    n, steps = len(plan), len(plan[0])

    def pick(values):
        def at(f):
            index = values[-1]
            for i in range(steps - 2, -1, -1):
                index = jnp.where(f == i, values[i], index)
            return 0, index

        return at

    across = (lambda f: (f, 0)) if stacked else (lambda f: (0, f))
    shape = (256 * steps, F) if stacked else (256, F * steps)
    return pl.pallas_call(
        functools.partial(parts_kernel, n),
        grid=(steps,),
        in_specs=[pl.BlockSpec((ROWS, 256), pick([b for b, _ in column])) for column in plan]
        + [pl.BlockSpec((ROWS, F), pick([g for _, g in plan[0]]))],
        out_specs=[pl.BlockSpec((256, F), across)] * n,
        out_shape=[jax.ShapeDtypeStruct(shape, dtype)] * n,
        cost_estimate=cost(2 * n * ROWS * 256 * steps * F, 2 * ROWS * steps * F),
        compiler_params=params(16),
    )(*([xs] * n), fac)


def weight_grads_of(xs, fac):
    far = parts(xs, fac, [[(4, 0)], [(5, 0)]], BF)
    far_r, far_l, xs, fac = together((*far, xs, fac))
    far_r, far_l = x_shift(far_r, 1), x_shift(far_l, -1)
    (cross,) = parts(xs, fac, [[(9, 2), (11, 2), (13, 2), (15, 2)]], BF, True)
    from_y = y_swap(cross)
    near_r, near_l = parts(xs, fac, [[(4, 1), (3, 0), (3, 1)], [(5, 1), (6, 0), (6, 1)]], BF)
    near_r, near_l = x_shift(near_r, 1), x_shift(near_l, -1)
    free = together((far_r, far_l, fac))[2]
    next_r, next_l, mine, away = parts(
        xs, fac, [[(2, 0), (2, 1)], [(7, 0), (7, 1)], [(0, 0), (0, 1)], [(1, 0), (1, 1)]], F32
    )
    (downs,) = parts(xs, fac, [[(8, 2), (10, 2), (12, 2), (14, 2)]], F32, True)

    def cols(value, g):
        return value[:, g * F : (g + 1) * F].astype(F32)

    fars = [(far_r, far_l), (near_r[:, :F], near_l[:, :F])]
    lasts = []
    for g in range(2):
        last_r = x_shift((cols(next_r, g) + fars[g][0].astype(F32)).astype(BF), 1)
        last_l = x_shift((cols(next_l, g) + fars[g][1].astype(F32)).astype(BF), -1)
        lasts.append((last_r.astype(F32), last_l.astype(F32)))
    down = downs + from_y.astype(F32)
    d0, d1, d2, d3 = [down[c * 256 : (c + 1) * 256] for c in range(4)]
    down_r = x_shift(jnp.concatenate([d2[:128], d1[128:]], axis=0).astype(BF), 1).astype(F32)
    down_l = x_shift(jnp.concatenate([d2[128:], d3[:128]], axis=0).astype(BF), -1).astype(F32)
    last_dr = x_shift((d1[:128] + down_r[:128]).astype(BF), 1).astype(F32)
    last_dl = x_shift((d3[128:] + down_l[:128]).astype(BF), -1).astype(F32)
    results = []
    for g in range(2):
        last_r, last_l = lasts[g]
        over = cols(away, g) + cols(near_r, g + 1) + last_l
        swapped = y_swap(over.astype(BF)).astype(F32)
        results.append(cols(mine, g) + cols(near_l, g + 1) + last_r + swapped)
    last = jnp.concatenate([down_l[128:] + last_dr, down_r[128:] + last_dl], axis=0)
    results.append(d0 + last)
    return jnp.concatenate(results, axis=1), free


def home_kernel(routes, probs, back, grads_out, probs_out):
    lane = lax.broadcasted_iota(I32, (T, ROWS), 1)
    expert = (lane // CAP).astype(F32)
    place = (lane % CAP).astype(F32)
    r = columns(routes[...])
    one, two = slots(r[:, 0:1], r[:, 1:2], expert, place)
    both = (one + two).astype(BF)
    grads_out[...] = jnp.dot(both, back[:, :D], preferred_element_type=F32).astype(BF)
    first = jnp.dot(one.astype(BF), back[:, D:], preferred_element_type=F32)
    second = jnp.dot(two.astype(BF), back[:, D:], preferred_element_type=F32)
    sums = [jnp.sum(first.T, axis=0, keepdims=True), jnp.sum(second.T, axis=0, keepdims=True)]
    probs_out[...] = jnp.concatenate(sums, axis=0) / probs[...].astype(F32)


def home_sums(routes, probs, back):
    return pl.pallas_call(
        home_kernel,
        out_shape=[jax.ShapeDtypeStruct((T, D), BF), jax.ShapeDtypeStruct((2, T), F32)],
        cost_estimate=cost(2 * ROWS * T * D, 2 * ROWS * D),
        compiler_params=params(16),
    )(routes.T, probs.T, back)


def shards(tokens, routes, gate_probs, cotangent, expert_weights):
    weights = expert_weights[0]

    home = pack(tokens, cotangent, routes, gate_probs)
    ahead, behind = [home], [home]
    for _ in range(2):
        ahead.append(z_shift(ahead[-1], 1))
        behind.append(z_shift(behind[-1], -1))

    def exchange(messages):
        return [messages[0]] + [plane_swap(messages[j], j) for j in range(1, NQ)]

    def order(ds):
        return [(d, j) for j in range(NQ) for d in ds]

    here = (0, 0, NQ)
    sel_a = select((here,) * 3, [home, ahead[1], behind[1]], True)
    two_r, two_l, sel_a = together((ahead[2], behind[2], sel_a))
    got_a = exchange(sel_a)
    held = expert_pass(weights, got_a, order((0, -1, 1)), 0, (), True)
    sel_b = select((here,) * 2, [ahead[2], behind[2]], True)
    three_r, three_l = z_shift(two_r, 1), z_shift(two_l, -1)
    three_r, three_l, held, sel_b = together((three_r, three_l, held, sel_b))
    got_b = exchange(sel_b)
    held = expert_pass(weights, got_b, order((-2, 2)), 3, held, True)

    for_four = select(((1, 0, 2), (-1, 2, 4)), [three_r, three_l], False)
    got_d = [diagonal(for_four[j], 1 if j < 2 else -1, j) for j in range(NQ)]
    for_four, three_r, three_l = together((for_four, three_r, three_l))
    got_c = exchange(select((here,) * 2, [three_r, three_l], True))
    last = order((-3, 3)) + order((4,))
    xs, fac, dots = expert_pass(weights, got_c + got_d, last, 1, held[:2], False)
    weight_grads, fac = weight_grads_of(xs, fac)

    rows = grad_pass(weights, fac, 1, dots, last, held[2])
    back = lax.all_to_all(
        rows.reshape(32, CAP, D + EXTRA), "expert", split_axis=0, concat_axis=0, tiled=True
    ).reshape(ROWS, D + EXTRA)
    token_grads, prob_grads = home_sums(routes, gate_probs, back)
    return token_grads, prob_grads.T, weight_grads[None]


def solution(mesh):
    rows = P(("dp", "expert"), None)
    return jax.shard_map(
        shards,
        mesh=mesh,
        in_specs=(rows, rows, rows, rows, P("expert", None, None)),
        out_specs=(rows, rows, P("expert", "dp", None)),
        check_vma=False,
    )
```

```python
import functools

import jax
import jax.numpy as jnp
from jax import lax
from jax.experimental import pallas as pl
from jax.experimental.pallas import tpu as pltpu
from jax.sharding import PartitionSpec as P

BF = jnp.bfloat16
F32 = jnp.float32
I32 = jnp.int32
D = 2048
F = 768
T = 128
CAP = 16
NZ = 8
NQ = 4
FB = 256
NF = F // FB
ROWS = NZ * NQ * CAP
EXTRA = 128
MIB = 1024 * 1024
NT = (((1,), (1,)), ((), ()))
TN = (((0,), (0,)), ((), ()))
ANY = pl.BlockSpec(memory_space=pl.ANY)
together = lax.optimization_barrier


def z_shift(value, step):
    return lax.ppermute(value, "expert", [(i, (i + NQ * step) % 32) for i in range(32)])


def plane_swap(value, mask):
    return lax.ppermute(value, "expert", [(i, i ^ mask) for i in range(32)])


def x_shift(value, step):
    return lax.ppermute(value, "dp", [(i, (i + 2 * step) % 8) for i in range(8)])


def y_swap(value):
    return lax.ppermute(value, "dp", [(i, i ^ 1) for i in range(8)])


def params(mib):
    return pltpu.CompilerParams(vmem_limit_bytes=mib * MIB)


def cost(flops, moved):
    return pl.CostEstimate(flops=flops // 1024, bytes_accessed=moved // 1024, transcendentals=0)


def columns(pairs):
    diagonal = lax.broadcasted_iota(I32, (T, T), 0) == lax.broadcasted_iota(I32, (T, T), 1)
    eye = diagonal.astype(F32).astype(BF)
    return lax.dot_general(eye, pairs.astype(F32).astype(BF), NT, preferred_element_type=F32)


def pack_kernel(tokens, cotangent, routes, probs, out):
    out[:, :D] = tokens[...]
    out[:, D : 2 * D] = cotangent[...]
    lane = lax.broadcasted_iota(I32, (T, EXTRA), 1)
    r, p = columns(routes[...]), columns(probs[...])
    meta = jnp.where(lane == 0, r[:, 0:1], jnp.where(lane == 1, r[:, 1:2], 0.0))
    meta += jnp.where(lane == 2, p[:, 0:1], jnp.where(lane == 3, p[:, 1:2], 0.0))
    out[:, 2 * D :] = meta.astype(BF)


def pack(tokens, cotangent, routes, probs):
    return pl.pallas_call(
        pack_kernel,
        out_shape=jax.ShapeDtypeStruct((T, 2 * D + EXTRA), BF),
        cost_estimate=cost(0, 4 * T * D * 2),
        compiler_params=params(8),
    )(tokens, cotangent, routes.T, probs.T)


def slots(r0, r1, expert, place):
    first = (r0 == expert).astype(F32)
    second = (r1 == expert).astype(F32)
    named = first + second
    row = lax.broadcasted_iota(I32, (T, T), 0)
    col = lax.broadcasted_iota(I32, (T, T), 1)
    before = (col < row).astype(F32).astype(BF)
    position = jnp.dot(before, named.astype(BF), preferred_element_type=F32)
    here = (position == place).astype(F32)
    return first * here, second * here


def select_kernel(plan, n, *refs):
    metas, ins, outs, hot = refs[:n], refs[n : 2 * n], refs[2 * n : -1], refs[-1]
    c = pl.program_id(0)

    @pl.when(c == 0)
    def _():
        me = lax.axis_index("expert")
        z, q = me // NQ, me % NQ
        for i, (block, step, _, _) in enumerate(plan):
            lane = lax.broadcasted_iota(I32, (T, NQ * CAP), 1)
            plane = (z + step + NZ) % NZ
            expert = (plane * NQ + jnp.bitwise_xor(q, lane // CAP)).astype(F32)
            place = (lane % CAP).astype(F32)
            meta = metas[block][...].astype(F32)
            one, two = slots(meta[:, 0:1], meta[:, 1:2], expert, place)
            hot[0, i] = (one + two).astype(BF)
            hot[1, i] = (one * meta[:, 2:3] + two * meta[:, 3:4]).astype(BF)

    for i, (block, _, experts, at) in enumerate(plan):
        rows = lax.dot_general(hot[c // 2, i], ins[block][...], TN, preferred_element_type=F32)
        rows = rows.astype(BF)
        for j in experts:
            outs[j][at : at + CAP, :] = rows[j * CAP : (j + 1) * CAP, :]


def select(plan, ins):
    n = len(ins)
    width = 1024
    height = max(at for _, _, _, at in plan) + CAP
    return pl.pallas_call(
        functools.partial(select_kernel, plan, n),
        grid=(2 * D // width,),
        in_specs=[pl.BlockSpec((T, EXTRA), lambda c: (0, 2 * D // EXTRA))] * n
        + [pl.BlockSpec((T, width), lambda c: (0, c))] * n,
        out_specs=[pl.BlockSpec((height, width), lambda c: (0, c))] * NQ,
        out_shape=[jax.ShapeDtypeStruct((height, 2 * D), BF)] * NQ,
        scratch_shapes=[pltpu.VMEM((2, len(plan), T, NQ * CAP), BF)],
        cost_estimate=cost(2 * n * 64 * T * 2 * D, n * 3 * T * D * 2),
        compiler_params=params(10),
    )(*ins, *ins)


def dot_columns(dots):
    lane = lax.broadcasted_iota(I32, dots.shape, 1)
    high = dots.astype(BF).astype(F32)
    return jnp.where(lane == 0, high, jnp.where(lane == 1, dots - high, 0.0)).astype(BF)


def place_rows(order, out_rows, grad_all, sems):
    me = lax.axis_index("expert")
    z, q = me // NQ, me % NQ
    copies = []
    for i, (step, near) in enumerate(order):
        owner = ((z + step + NZ) % NZ) * NQ + jnp.bitwise_xor(q, near)
        copies.append(
            pltpu.make_async_copy(
                out_rows.at[pl.ds(i * CAP, CAP)],
                grad_all.at[pl.ds(pl.multiple_of(owner * CAP, CAP), CAP)],
                sems.at[i],
            )
        )
    for copy in copies:
        copy.start()
    for copy in copies:
        copy.wait()


def expert_kernel(pieces, order, grads, aliased, gate_w, up_w, down_w, *refs):
    ins = refs[: len(pieces)]
    refs = refs[len(pieces) + aliased :]
    if grads:
        xs, fac, grad_all, rows, dot_acc, acc, out_rows, sems = refs
    else:
        xs, fac, dots, rows, dot_acc = refs
    f = pl.program_id(0)

    @pl.when(f == 0)
    def _():
        at = 0
        for size, ref in zip(pieces, ins):
            rows[at : at + size, :] = ref[...]
            at += size
        dot_acc[...] = jnp.zeros_like(dot_acc)
        if grads:
            acc[...] = jnp.zeros_like(acc)

    x = rows[:, :D]
    gate = jnp.dot(x, gate_w[...], preferred_element_type=F32)
    up = jnp.dot(x, up_w[...], preferred_element_type=F32)
    dh = jnp.dot(rows[:, D:], down_w[...], preferred_element_type=F32)
    sig = jax.nn.sigmoid(gate)
    active = gate * sig
    hidden = (active * up).astype(BF)
    d_gate = (dh * up * sig * (1.0 + gate * (1.0 - sig))).astype(BF)
    d_up = (dh * active).astype(BF)
    at = pl.multiple_of(f * FB, FB)
    fac[:, pl.ds(at, FB)] = d_gate
    fac[:, pl.ds(F + at, FB)] = d_up
    fac[:, pl.ds(2 * F + at, FB)] = hidden
    prod = hidden.astype(F32) * dh
    dot_acc[...] += prod[:, :128] + prod[:, 128:]
    if grads:
        acc[...] += lax.dot_general(d_gate, gate_w[...], NT, preferred_element_type=F32)
        acc[...] += lax.dot_general(d_up, up_w[...], NT, preferred_element_type=F32)

    @pl.when(f == NF - 1)
    def _():
        dp = lax.axis_index("dp")
        xi, yi = dp // 2, dp % 2
        for part in range(2):
            for chunk in range(4):
                for half in range(2):
                    source = ((xi + chunk) % 4) * 2 + jnp.bitwise_xor(yi, half)
                    source = pl.multiple_of(part * D + source * 256, 256)
                    to = part * D + (chunk * 2 + half) * 256
                    xs[:, to : to + 256] = rows[:, pl.ds(source, 256)]
        total = jnp.sum(dot_acc[...], axis=1, keepdims=True)
        total = jnp.broadcast_to(total, dot_acc.shape)
        if grads:
            out_rows[:, :D] = acc[...].astype(BF)
            out_rows[:, D:] = dot_columns(total)
            place_rows(order, out_rows, grad_all, sems)
        else:
            dots[...] = total


def expert_pass(weights, pieces, sizes, order, block, held, grads):
    rows = sum(sizes)
    whole = lambda f: (0, 0)
    mine = lambda f: (block, 0)
    outs = [pl.BlockSpec((rows, 2 * D), mine), pl.BlockSpec((rows, 3 * F), mine)]
    shapes = [jax.ShapeDtypeStruct((ROWS, 2 * D), BF), jax.ShapeDtypeStruct((ROWS, 3 * F), BF)]
    scratch = [pltpu.VMEM((rows, 2 * D), BF), pltpu.VMEM((rows, 128), F32)]
    if grads:
        outs.append(ANY)
        shapes.append(jax.ShapeDtypeStruct((ROWS, D + EXTRA), BF))
        scratch += [
            pltpu.VMEM((rows, D), F32),
            pltpu.VMEM((rows, D + EXTRA), BF),
            pltpu.SemaphoreType.DMA((rows // CAP,)),
        ]
    else:
        outs.append(pl.BlockSpec((rows, 128), whole))
        shapes.append(jax.ShapeDtypeStruct((rows, 128), F32))
    return pl.pallas_call(
        functools.partial(expert_kernel, sizes, order, grads, len(held)),
        grid=(NF,),
        in_specs=[
            pl.BlockSpec((D, FB), lambda f: (0, f)),
            pl.BlockSpec((D, FB), lambda f: (0, f + NF)),
            pl.BlockSpec((D, FB), lambda f: (0, f + 2 * NF)),
        ]
        + [pl.BlockSpec((size, 2 * D), whole) for size in sizes]
        + [ANY] * len(held),
        out_specs=outs,
        out_shape=shapes,
        scratch_shapes=scratch,
        input_output_aliases={3 + len(pieces) + i: i for i in range(len(held))},
        cost_estimate=cost(2 * rows * D * (5 if grads else 3) * F, D * 3 * F * 2),
        compiler_params=params(24),
    )(weights, weights, weights, *pieces, *held)


def grad_kernel(order, gate_w, up_w, gate_f, up_f, dots, held, grad_all, acc, out_rows, sems):
    f = pl.program_id(0)

    @pl.when(f == 0)
    def _():
        acc[...] = jnp.zeros_like(acc)

    acc[...] += lax.dot_general(gate_f[...], gate_w[...], NT, preferred_element_type=F32)
    acc[...] += lax.dot_general(up_f[...], up_w[...], NT, preferred_element_type=F32)

    @pl.when(f == NF - 1)
    def _():
        out_rows[:, :D] = acc[...].astype(BF)
        out_rows[:, D:] = dot_columns(dots[...])
        place_rows(order, out_rows, grad_all, sems)


def grad_pass(weights, fac, block, dots, order, grad_all):
    rows = dots.shape[0]
    return pl.pallas_call(
        functools.partial(grad_kernel, order),
        grid=(NF,),
        in_specs=[
            pl.BlockSpec((D, FB), lambda f: (0, f)),
            pl.BlockSpec((D, FB), lambda f: (0, f + NF)),
            pl.BlockSpec((rows, FB), lambda f: (block, f)),
            pl.BlockSpec((rows, FB), lambda f: (block, f + NF)),
            pl.BlockSpec((rows, 128), lambda f: (0, 0)),
            ANY,
        ],
        out_specs=ANY,
        out_shape=jax.ShapeDtypeStruct(grad_all.shape, BF),
        scratch_shapes=[
            pltpu.VMEM((rows, D), F32),
            pltpu.VMEM((rows, D + EXTRA), BF),
            pltpu.SemaphoreType.DMA((rows // CAP,)),
        ],
        input_output_aliases={5: 0},
        cost_estimate=cost(4 * rows * D * F, D * 2 * F * 2),
        compiler_params=params(20),
    )(weights, weights, fac, fac, dots, grad_all)


def parts_kernel(counts, *refs):
    n = len(counts)
    fac = refs[n][...]
    adds, outs = refs[n + 1 : n + 1 + sum(counts)], refs[-n:]
    for i, count in enumerate(counts):
        total = lax.dot_general(refs[i][...], fac, TN, preferred_element_type=F32)
        for ref in adds[:count]:
            total += ref[...].astype(F32)
        adds = adds[count:]
        outs[i][...] = total.astype(outs[i].dtype)


def parts(xs, fac, plan, dtype, adds=None, into=None, weight=1):
    n, steps = len(plan), len(plan[0])
    adds = adds or [()] * n

    def pick(values):
        def at(f):
            index = values[-1]
            for i in range(steps - 2, -1, -1):
                index = jnp.where(f == i, values[i], index)
            return 0, index

        return at

    def side(first):
        return pl.BlockSpec((256, F), lambda f: (0, f + first))

    flat = [add for some in adds for add in some]
    held = [] if into is None or into is True else [into]
    group, total = (0, steps) if into is None else (plan[0][0][1], 3)
    return pl.pallas_call(
        functools.partial(parts_kernel, [len(some) for some in adds]),
        grid=(steps,),
        in_specs=[pl.BlockSpec((ROWS, 256), pick([b for b, _ in column])) for column in plan]
        + [pl.BlockSpec((ROWS, F), pick([g for _, g in plan[0]]))]
        + [side(first) for _, first in flat]
        + [ANY] * len(held),
        out_specs=[side(group)] * n,
        out_shape=[jax.ShapeDtypeStruct((256, F * total), dtype)] * n,
        input_output_aliases={n + 1 + len(flat): 0} if held else {},
        cost_estimate=cost(weight * 2 * n * ROWS * 256 * steps * F, 2 * ROWS * steps * F),
        compiler_params=params(16),
    )(*([xs] * n), fac, *[value for value, _ in flat], *held)


def weight_grads_of(xs, fac, finish):
    far = parts(xs, fac, [[(4, 0)], [(5, 0)]], BF)
    far_r, far_l, xs, fac = together((*far, xs, fac))
    far_r, far_l = x_shift(far_r, 1), x_shift(far_l, -1)
    near = parts(
        xs,
        fac,
        [
            [(4, 1), (12, 2), (3, 0), (3, 1), (11, 2)],
            [(5, 1), (13, 2), (6, 0), (6, 1), (14, 2)],
        ],
        BF,
    )
    *near, fac = together((*near, fac))
    near_r, near_l = together((x_shift(near[0], 1), x_shift(near[1], -1)))
    far_r, far_l, free = together((far_r, far_l, fac))
    rows = finish(free)
    last = parts(xs, fac, [[(2, 0)], [(7, 0)]], BF, [[(far_r, 0)], [(far_l, 0)]], None, 100000)
    lasts = [together((x_shift(last[0], 1), x_shift(last[1], -1)))]
    for group, block in ((1, 0), (2, 8)):
        last = parts(
            xs,
            fac,
            [[(2 + block, group)], [(7 + block, group)]],
            BF,
            [[(near_r, group - 1)], [(near_l, group - 1)]],
        )
        lasts.append(together((x_shift(last[0], 1), x_shift(last[1], -1))))
    result = True
    for group, block in ((0, 0), (1, 0), (2, 8)):
        last_r, last_l = lasts[group]
        beside = 2 + group
        (over,) = parts(
            xs, fac, [[(1 + block, group)]], BF, [[(near_r, beside), (last_l, 0)]]
        )
        swapped = y_swap(over)
        adds = [[(near_l, beside), (last_r, 0), (swapped, 0)]]
        (result,) = parts(xs, fac, [[(block, group)]], F32, adds, result)
    return result, rows


def home_kernel(routes, probs, back, grads_out, probs_out):
    lane = lax.broadcasted_iota(I32, (T, ROWS), 1)
    expert = (lane // CAP).astype(F32)
    place = (lane % CAP).astype(F32)
    r = columns(routes[...])
    one, two = slots(r[:, 0:1], r[:, 1:2], expert, place)
    both = (one + two).astype(BF)
    grads_out[...] = jnp.dot(both, back[:, :D], preferred_element_type=F32).astype(BF)
    first = jnp.dot(one.astype(BF), back[:, D:], preferred_element_type=F32)
    second = jnp.dot(two.astype(BF), back[:, D:], preferred_element_type=F32)
    sums = [jnp.sum(first.T, axis=0, keepdims=True), jnp.sum(second.T, axis=0, keepdims=True)]
    probs_out[...] = jnp.concatenate(sums, axis=0) / probs[...].astype(F32)


def home_sums(routes, probs, back):
    return pl.pallas_call(
        home_kernel,
        out_shape=[jax.ShapeDtypeStruct((T, D), BF), jax.ShapeDtypeStruct((2, T), F32)],
        cost_estimate=cost(2 * ROWS * T * D, 2 * ROWS * D),
        compiler_params=params(16),
    )(routes.T, probs.T, back)


def shards(tokens, routes, gate_probs, cotangent, expert_weights):
    weights = expert_weights[0]

    home = pack(tokens, cotangent, routes, gate_probs)
    ahead, behind = [home], [home]
    for _ in range(2):
        ahead.append(z_shift(ahead[-1], 1))
        behind.append(z_shift(behind[-1], -1))

    def exchange(messages):
        return [messages[0]] + [plane_swap(messages[j], j) for j in range(1, NQ)]

    def order(ds):
        return [(d, j) for j in range(NQ) for d in ds]

    every = tuple(range(NQ))
    sel_a = select([(i, 0, every, i * CAP) for i in range(3)], [home, ahead[1], behind[1]])
    got_a = exchange(sel_a)
    halfway = [(0, 2, (0, 1), 2 * CAP), (1, -2, (2, 3), 2 * CAP)]
    pair = [(i, 0, every, i * CAP) for i in range(2)]
    got_b = exchange(select(pair + halfway, [ahead[2], behind[2]]))
    two_l, got_a = together((behind[2], got_a))
    three_r, three_l = z_shift(ahead[2], 1), z_shift(two_l, -1)
    held = expert_pass(weights, got_a, [3 * CAP] * NQ, order((0, -1, 1)), 0, (), True)
    three_r, three_l, held, got_b = together((three_r, three_l, held, got_b))
    got_c = exchange(select(pair, [three_r, three_l]))
    across = [piece[2 * CAP :] for piece in got_b]
    four_r = z_shift(jnp.concatenate(across[:2], axis=0), 2)
    four_l = z_shift(jnp.concatenate(across[2:], axis=0), -2)
    held = expert_pass(weights, got_b, [2 * CAP] * NQ, order((-2, 2)), 3, held, True)
    last = order((-3, 3)) + order((4,))
    pieces = got_c + [four_r, four_l]
    xs, fac, dots = expert_pass(weights, pieces, [2 * CAP] * 6, last, 1, held[:2], False)
    weight_grads, rows = weight_grads_of(
        xs, fac, lambda f: grad_pass(weights, f, 1, dots, last, held[2])
    )

    back = lax.all_to_all(
        rows.reshape(32, CAP, D + EXTRA), "expert", split_axis=0, concat_axis=0, tiled=True
    ).reshape(ROWS, D + EXTRA)
    token_grads, prob_grads = home_sums(routes, gate_probs, back)
    return token_grads, prob_grads.T, weight_grads[None]


def solution(mesh):
    rows = P(("dp", "expert"), None)
    return jax.shard_map(
        shards,
        mesh=mesh,
        in_specs=(rows, rows, rows, rows, P("expert", None, None)),
        out_specs=(rows, rows, P("expert", "dp", None)),
        check_vma=False,
    )
```

```python
import functools

import jax
import jax.numpy as jnp
from jax import lax
from jax.experimental import pallas as pl
from jax.experimental.pallas import tpu as pltpu
from jax.sharding import PartitionSpec as P

BF = jnp.bfloat16
F32 = jnp.float32
I32 = jnp.int32
D = 2048
F = 768
T = 128
CAP = 16
NZ = 8
NQ = 4
FB = 256
NF = F // FB
ROWS = NZ * NQ * CAP
EXTRA = 128
MIB = 1024 * 1024
NT = (((1,), (1,)), ((), ()))
TN = (((0,), (0,)), ((), ()))
ANY = pl.BlockSpec(memory_space=pl.ANY)
together = lax.optimization_barrier


def z_shift(value, step, mask=0):
    return lax.ppermute(value, "expert", [(i, ((i ^ mask) + NQ * step) % 32) for i in range(32)])


def plane_swap(value, mask):
    return lax.ppermute(value, "expert", [(i, i ^ mask) for i in range(32)])


def x_shift(value, step):
    return lax.ppermute(value, "dp", [(i, (i + 2 * step) % 8) for i in range(8)])


def y_swap(value):
    return lax.ppermute(value, "dp", [(i, i ^ 1) for i in range(8)])


def params(mib):
    return pltpu.CompilerParams(vmem_limit_bytes=mib * MIB)


def cost(flops, moved):
    return pl.CostEstimate(flops=flops // 1024, bytes_accessed=moved // 1024, transcendentals=0)


def columns(pairs):
    diagonal = lax.broadcasted_iota(I32, (T, T), 0) == lax.broadcasted_iota(I32, (T, T), 1)
    eye = diagonal.astype(F32).astype(BF)
    return lax.dot_general(eye, pairs.astype(F32).astype(BF), NT, preferred_element_type=F32)


def pack_kernel(tokens, cotangent, routes, probs, out, pairs, weights, meta, sems):
    loads = [
        pltpu.make_async_copy(routes, pairs, sems.at[0]),
        pltpu.make_async_copy(probs, weights, sems.at[1]),
    ]
    rows = [
        pltpu.make_async_copy(tokens, out.at[:, pl.ds(0, D)], sems.at[2]),
        pltpu.make_async_copy(cotangent, out.at[:, pl.ds(D, D)], sems.at[3]),
    ]
    for copy in loads + rows:
        copy.start()
    for copy in loads:
        copy.wait()
    lane = lax.broadcasted_iota(I32, (T, EXTRA), 1)
    r, p = columns(pairs[...]), columns(weights[...])
    value = jnp.where(lane == 0, r[:, 0:1], jnp.where(lane == 1, r[:, 1:2], 0.0))
    value += jnp.where(lane == 2, p[:, 0:1], jnp.where(lane == 3, p[:, 1:2], 0.0))
    meta[...] = value.astype(BF)
    last = pltpu.make_async_copy(meta, out.at[:, pl.ds(2 * D, EXTRA)], sems.at[4])
    last.start()
    last.wait()
    for copy in rows:
        copy.wait()


def pack(tokens, cotangent, routes, probs):
    return pl.pallas_call(
        pack_kernel,
        in_specs=[ANY] * 4,
        out_specs=ANY,
        out_shape=jax.ShapeDtypeStruct((T, 2 * D + EXTRA), BF),
        scratch_shapes=[
            pltpu.VMEM((2, T), I32),
            pltpu.VMEM((2, T), BF),
            pltpu.VMEM((T, EXTRA), BF),
            pltpu.SemaphoreType.DMA((5,)),
        ],
        cost_estimate=cost(0, 8 * T * D),
        compiler_params=params(8),
    )(tokens, cotangent, routes.T, probs.T)


def slots(r0, r1, expert, place):
    first = (r0 == expert).astype(F32)
    second = (r1 == expert).astype(F32)
    named = first + second
    row = lax.broadcasted_iota(I32, (T, T), 0)
    col = lax.broadcasted_iota(I32, (T, T), 1)
    before = (col < row).astype(F32).astype(BF)
    position = jnp.dot(before, named.astype(BF), preferred_element_type=F32)
    here = (position == place).astype(F32)
    return first * here, second * here


def select_kernel(plan, n, *refs):
    metas, ins = refs[:n], refs[n : 2 * n]
    outs, hot = refs[2 * n : -1], refs[-1]
    c = pl.program_id(0)

    @pl.when(c == 0)
    def _():
        me = lax.axis_index("expert")
        z, q = me // NQ, me % NQ
        for i, (block, step, _) in enumerate(plan):
            lane = lax.broadcasted_iota(I32, (T, NQ * CAP), 1)
            plane = (z + step + NZ) % NZ
            expert = (plane * NQ + jnp.bitwise_xor(q, lane // CAP)).astype(F32)
            place = (lane % CAP).astype(F32)
            meta = metas[block][...].astype(F32)
            one, two = slots(meta[:, 0:1], meta[:, 1:2], expert, place)
            hot[0, i] = (one + two).astype(BF)
            hot[1, i] = (one * meta[:, 2:3] + two * meta[:, 3:4]).astype(BF)

    for i, (block, _, targets) in enumerate(plan):
        rows = lax.dot_general(hot[c // 2, i], ins[block][...], TN, preferred_element_type=F32)
        rows = rows.astype(BF)
        for j, out, at in targets:
            outs[out][at : at + CAP, :] = rows[j * CAP : (j + 1) * CAP, :]


def select(plan, ins, heights):
    n = len(ins)
    width = 1024
    return pl.pallas_call(
        functools.partial(select_kernel, plan, n),
        grid=(2 * D // width,),
        in_specs=[pl.BlockSpec((T, EXTRA), lambda c: (0, 2 * D // EXTRA))] * n
        + [pl.BlockSpec((T, width), lambda c: (0, c))] * n,
        out_specs=[pl.BlockSpec((height, width), lambda c: (0, c)) for height in heights],
        out_shape=[jax.ShapeDtypeStruct((height, 2 * D), BF) for height in heights],
        scratch_shapes=[pltpu.VMEM((2, len(plan), T, NQ * CAP), BF)],
        cost_estimate=cost(2 * n * 64 * T * 2 * D, n * 3 * T * D * 2),
        compiler_params=params(12),
    )(*ins, *ins)


def dot_columns(dots):
    lane = lax.broadcasted_iota(I32, dots.shape, 1)
    high = dots.astype(BF).astype(F32)
    return jnp.where(lane == 0, high, jnp.where(lane == 1, dots - high, 0.0)).astype(BF)


def place_rows(order, out_rows, grad_all, sems):
    me = lax.axis_index("expert")
    z, q = me // NQ, me % NQ
    copies = []
    for i, (step, near) in enumerate(order):
        owner = ((z + step + NZ) % NZ) * NQ + jnp.bitwise_xor(q, near)
        copies.append(
            pltpu.make_async_copy(
                out_rows.at[pl.ds(i * CAP, CAP)],
                grad_all.at[pl.ds(pl.multiple_of(owner * CAP, CAP), CAP)],
                sems.at[i],
            )
        )
    for copy in copies:
        copy.start()
    for copy in copies:
        copy.wait()


def expert_kernel(pieces, order, grads, aliased, gate_w, up_w, down_w, *refs):
    ins = refs[: len(pieces)]
    refs = refs[len(pieces) + aliased :]
    if grads:
        xs, fac, grad_all, rows, dot_acc, acc, out_rows, sems = refs
    else:
        xs, fac, dots, rows, dot_acc = refs
    f = pl.program_id(0)

    @pl.when(f == 0)
    def _():
        at = 0
        for size, ref in zip(pieces, ins):
            rows[at : at + size, :] = ref[...]
            at += size
        dot_acc[...] = jnp.zeros_like(dot_acc)
        if grads:
            acc[...] = jnp.zeros_like(acc)

    x = rows[:, :D]
    gate = jnp.dot(x, gate_w[...], preferred_element_type=F32)
    up = jnp.dot(x, up_w[...], preferred_element_type=F32)
    dh = jnp.dot(rows[:, D:], down_w[...], preferred_element_type=F32)
    sig = jax.nn.sigmoid(gate)
    active = gate * sig
    hidden = (active * up).astype(BF)
    d_gate = (dh * up * sig * (1.0 + gate * (1.0 - sig))).astype(BF)
    d_up = (dh * active).astype(BF)
    at = pl.multiple_of(f * FB, FB)
    fac[:, pl.ds(at, FB)] = d_gate
    fac[:, pl.ds(F + at, FB)] = d_up
    fac[:, pl.ds(2 * F + at, FB)] = hidden
    prod = hidden.astype(F32) * dh
    dot_acc[...] += prod[:, :128] + prod[:, 128:]
    if grads:
        acc[...] += lax.dot_general(d_gate, gate_w[...], NT, preferred_element_type=F32)
        acc[...] += lax.dot_general(d_up, up_w[...], NT, preferred_element_type=F32)

    @pl.when(f == NF - 1)
    def _():
        dp = lax.axis_index("dp")
        xi, yi = dp // 2, dp % 2
        for part in range(2):
            for chunk in range(4):
                for half in range(2):
                    source = ((xi + chunk) % 4) * 2 + jnp.bitwise_xor(yi, half)
                    source = pl.multiple_of(part * D + source * 256, 256)
                    to = part * D + (chunk * 2 + half) * 256
                    xs[:, to : to + 256] = rows[:, pl.ds(source, 256)]
        total = jnp.sum(dot_acc[...], axis=1, keepdims=True)
        total = jnp.broadcast_to(total, dot_acc.shape)
        if grads:
            out_rows[:, :D] = acc[...].astype(BF)
            out_rows[:, D:] = dot_columns(total)
            place_rows(order, out_rows, grad_all, sems)
        else:
            dots[...] = total


def expert_pass(weights, pieces, order, block, held, grads):
    sizes = [size for _, size, _ in pieces]
    rows = sum(sizes)
    whole = lambda f: (0, 0)
    mine = lambda f: (block, 0)
    outs = [pl.BlockSpec((rows, 2 * D), mine), pl.BlockSpec((rows, 3 * F), mine)]
    shapes = [jax.ShapeDtypeStruct((ROWS, 2 * D), BF), jax.ShapeDtypeStruct((ROWS, 3 * F), BF)]
    scratch = [pltpu.VMEM((rows, 2 * D), BF), pltpu.VMEM((rows, 128), F32)]
    if grads:
        outs.append(ANY)
        shapes.append(jax.ShapeDtypeStruct((ROWS, D + EXTRA), BF))
        scratch += [
            pltpu.VMEM((rows, D), F32),
            pltpu.VMEM((rows, D + EXTRA), BF),
            pltpu.SemaphoreType.DMA((rows // CAP,)),
        ]
    else:
        outs.append(pl.BlockSpec((rows, 128), whole))
        shapes.append(jax.ShapeDtypeStruct((rows, 128), F32))
    return pl.pallas_call(
        functools.partial(expert_kernel, sizes, order, grads, len(held)),
        grid=(NF,),
        in_specs=[
            pl.BlockSpec((D, FB), lambda f: (0, f)),
            pl.BlockSpec((D, FB), lambda f: (0, f + NF)),
            pl.BlockSpec((D, FB), lambda f: (0, f + 2 * NF)),
        ]
        + [pl.BlockSpec((size, 2 * D), (lambda f, at=at: (at, 0))) for _, size, at in pieces]
        + [ANY] * len(held),
        out_specs=outs,
        out_shape=shapes,
        scratch_shapes=scratch,
        input_output_aliases={3 + len(pieces) + i: i for i in range(len(held))},
        cost_estimate=cost(2 * rows * D * (5 if grads else 3) * F, D * 3 * F * 2),
        compiler_params=params(24),
    )(weights, weights, weights, *[piece for piece, _, _ in pieces], *held)


def grad_kernel(order, gate_w, up_w, gate_f, up_f, dots, held, grad_all, acc, out_rows, sems):
    f = pl.program_id(0)

    @pl.when(f == 0)
    def _():
        acc[...] = jnp.zeros_like(acc)

    acc[...] += lax.dot_general(gate_f[...], gate_w[...], NT, preferred_element_type=F32)
    acc[...] += lax.dot_general(up_f[...], up_w[...], NT, preferred_element_type=F32)

    @pl.when(f == NF - 1)
    def _():
        out_rows[:, :D] = acc[...].astype(BF)
        out_rows[:, D:] = dot_columns(dots[...])
        place_rows(order, out_rows, grad_all, sems)


def grad_pass(weights, fac, block, dots, order, grad_all):
    rows = dots.shape[0]
    return pl.pallas_call(
        functools.partial(grad_kernel, order),
        grid=(NF,),
        in_specs=[
            pl.BlockSpec((D, FB), lambda f: (0, f)),
            pl.BlockSpec((D, FB), lambda f: (0, f + NF)),
            pl.BlockSpec((rows, FB), lambda f: (block, f)),
            pl.BlockSpec((rows, FB), lambda f: (block, f + NF)),
            pl.BlockSpec((rows, 128), lambda f: (0, 0)),
            ANY,
        ],
        out_specs=ANY,
        out_shape=jax.ShapeDtypeStruct(grad_all.shape, BF),
        scratch_shapes=[
            pltpu.VMEM((rows, D), F32),
            pltpu.VMEM((rows, D + EXTRA), BF),
            pltpu.SemaphoreType.DMA((rows // CAP,)),
        ],
        input_output_aliases={5: 0},
        cost_estimate=cost(4 * rows * D * F, D * 2 * F * 2),
        compiler_params=params(20),
    )(weights, weights, fac, fac, dots, grad_all)


def parts_kernel(counts, *refs):
    n = len(counts)
    fac = refs[n][...]
    adds, outs = refs[n + 1 : n + 1 + sum(counts)], refs[-n:]
    for i, count in enumerate(counts):
        total = lax.dot_general(refs[i][...], fac, TN, preferred_element_type=F32)
        for ref in adds[:count]:
            total += ref[...].astype(F32)
        adds = adds[count:]
        outs[i][...] = total.astype(outs[i].dtype)


def parts(xs, fac, plan, dtype, adds=None, into=None, weight=1):
    n, steps = len(plan), len(plan[0])
    adds = adds or [()] * n

    def pick(values):
        def at(f):
            index = values[-1]
            for i in range(steps - 2, -1, -1):
                index = jnp.where(f == i, values[i], index)
            return 0, index

        return at

    def side(first):
        return pl.BlockSpec((256, F), lambda f: (0, f + first))

    flat = [add for some in adds for add in some]
    held = [] if into is None or into is True else [into]
    group, total = (0, steps) if into is None else (plan[0][0][1], 3)
    return pl.pallas_call(
        functools.partial(parts_kernel, [len(some) for some in adds]),
        grid=(steps,),
        in_specs=[pl.BlockSpec((ROWS, 256), pick([b for b, _ in column])) for column in plan]
        + [pl.BlockSpec((ROWS, F), pick([g for _, g in plan[0]]))]
        + [side(first) for _, first in flat]
        + [ANY] * len(held),
        out_specs=[side(group)] * n,
        out_shape=[jax.ShapeDtypeStruct((256, F * total), dtype)] * n,
        input_output_aliases={n + 1 + len(flat): 0} if held else {},
        cost_estimate=cost(weight * 2 * n * ROWS * 256 * steps * F, 2 * ROWS * steps * F),
        compiler_params=params(16),
    )(*([xs] * n), fac, *[value for value, _ in flat], *held)


def total_kernel(n, *refs):
    value = refs[0][...].astype(F32)
    for ref in refs[1:n]:
        value += ref[...].astype(F32)
    refs[-1][...] = value.astype(refs[-1].dtype)


def total(adds, dtype, group=0, into=None):
    n = len(adds)
    held = [] if into is None or into is True else [into]
    return pl.pallas_call(
        functools.partial(total_kernel, n),
        grid=(2,),
        in_specs=[
            pl.BlockSpec((256, F // 2), lambda f, at=at: (0, 2 * at + f)) for _, at in adds
        ]
        + [ANY] * len(held),
        out_specs=pl.BlockSpec((256, F // 2), lambda f: (0, 2 * group + f)),
        out_shape=jax.ShapeDtypeStruct((256, F if into is None else 3 * F), dtype),
        input_output_aliases={n: 0} if held else {},
        cost_estimate=cost(n * 256 * F, n * 512 * F),
        compiler_params=params(8),
    )(*[value for value, _ in adds], *held)


def weight_grads_of(xs, fac, finish):
    far = parts(xs, fac, [[(4, 0)], [(5, 0)]], BF)
    far_r, far_l, xs, fac = together((*far, xs, fac))
    far_r, far_l = x_shift(far_r, 1), x_shift(far_l, -1)
    near = parts(
        xs,
        fac,
        [
            [(4, 1), (12, 2), (3, 0), (3, 1), (11, 2)],
            [(5, 1), (13, 2), (6, 0), (6, 1), (14, 2)],
        ],
        BF,
    )
    *near, fac = together((*near, fac))
    near_r, near_l = together((x_shift(near[0], 1), x_shift(near[1], -1)))
    far_r, far_l, free = together((far_r, far_l, fac))
    homes = finish(free)
    last = parts(xs, fac, [[(2, 0)], [(7, 0)]], BF, [[(far_r, 0)], [(far_l, 0)]], None, 100000)
    lasts = [together((x_shift(last[0], 1), x_shift(last[1], -1)))]
    for group, block in ((1, 0), (2, 8)):
        last = parts(
            xs,
            fac,
            [[(2 + block, group)], [(7 + block, group)]],
            BF,
            [[(near_r, group - 1)], [(near_l, group - 1)]],
        )
        lasts.append(together((x_shift(last[0], 1), x_shift(last[1], -1))))
    mine, away = parts(xs, fac, [[(0, 0), (0, 1), (8, 2)], [(1, 0), (1, 1), (9, 2)]], BF)
    result = True
    for group in range(3):
        last_r, last_l = lasts[group]
        over = total([(away, group), (near_r, 2 + group), (last_l, 0)], BF)
        swapped = y_swap(over)
        if group == 2:
            swapped, homes = together((swapped, homes))
        adds = [(mine, group), (near_l, 2 + group), (last_r, 0), (swapped, 0)]
        result = total(adds, F32, group, result)
    return result, homes


def home_kernel(routes, probs, back, grads_out, probs_out):
    lane = lax.broadcasted_iota(I32, (T, ROWS), 1)
    expert = (lane // CAP).astype(F32)
    place = (lane % CAP).astype(F32)
    r = columns(routes[...])
    one, two = slots(r[:, 0:1], r[:, 1:2], expert, place)
    both = (one + two).astype(BF)
    grads_out[...] = jnp.dot(both, back[:, :D], preferred_element_type=F32).astype(BF)
    first = jnp.dot(one.astype(BF), back[:, D:], preferred_element_type=F32)
    second = jnp.dot(two.astype(BF), back[:, D:], preferred_element_type=F32)
    sums = [jnp.sum(first.T, axis=0, keepdims=True), jnp.sum(second.T, axis=0, keepdims=True)]
    probs_out[...] = jnp.concatenate(sums, axis=0) / probs[...].astype(F32)


def home_sums(routes, probs, back):
    return pl.pallas_call(
        home_kernel,
        out_shape=[jax.ShapeDtypeStruct((T, D), BF), jax.ShapeDtypeStruct((2, T), F32)],
        cost_estimate=cost(2 * ROWS * T * D, 2 * ROWS * D),
        compiler_params=params(16),
    )(routes.T, probs.T, back)


def shards(tokens, routes, gate_probs, cotangent, expert_weights):
    weights = expert_weights[0]

    home = pack(tokens, cotangent, routes, gate_probs)
    ahead, behind = [home], [home]
    for _ in range(2):
        ahead.append(z_shift(ahead[-1], 1))
        behind.append(z_shift(behind[-1], -1))

    def exchange(messages):
        return [messages[0]] + [plane_swap(messages[j], j) for j in range(1, NQ)]

    def order(ds):
        return [(d, j) for j in range(NQ) for d in ds]

    def each(at):
        return [(j, j, at) for j in range(NQ)]

    def whole_of(pieces, rows):
        return [(piece, rows, 0) for piece in pieces]

    sel_a = select(
        [(i, 0, each(i * CAP)) for i in range(3)], [home, ahead[1], behind[1]], [48] * NQ
    )
    got_a = exchange(sel_a)
    two_l, got_a = together((behind[2], got_a))
    plan = [
        (0, 0, each(0)),
        (1, 0, each(CAP)),
        (0, 2, [(0, 0, 32), (1, 1, 32)]),
        (1, -2, [(2, 2, 32), (3, 3, 32)]),
        (0, 1, [(j, 4, j * CAP) for j in range(NQ)]),
        (1, -1, [(j, 5, j * CAP) for j in range(NQ)]),
    ]
    *sel_b, on_r, on_l = select(plan, [ahead[2], two_l], [48] * NQ + [64] * 2)
    three_r, three_l = z_shift(on_r, 1), z_shift(on_l, -1)
    got_b = exchange(sel_b)
    held = expert_pass(weights, whole_of(got_a, 48), order((0, -1, 1)), 0, (), True)
    three_r, three_l, held = together((three_r, three_l, held))
    got_c = exchange(
        [
            jnp.concatenate([v[j * CAP : (j + 1) * CAP] for v in (three_r, three_l)], axis=0)
            for j in range(NQ)
        ]
    )
    across = [piece[2 * CAP :] for piece in got_b]
    four_r = z_shift(jnp.concatenate(across[:2], axis=0), 2)
    four_l = z_shift(jnp.concatenate(across[2:], axis=0), -2)
    held = expert_pass(weights, whole_of(got_b, 32), order((-2, 2)), 3, held, True)
    last = order((-3, 3)) + order((4,))
    pieces = whole_of(got_c + [four_r, four_l], 32)
    xs, fac, dots = expert_pass(weights, pieces, last, 1, held[:2], False)
    def finish(factors):
        rows = grad_pass(weights, factors, 1, dots, last, held[2])
        back = lax.all_to_all(
            rows.reshape(32, CAP, D + EXTRA), "expert", split_axis=0, concat_axis=0, tiled=True
        ).reshape(ROWS, D + EXTRA)
        return home_sums(routes, gate_probs, back)

    weight_grads, homes = weight_grads_of(xs, fac, finish)
    token_grads, prob_grads = homes
    return token_grads, prob_grads.T, weight_grads[None]


def solution(mesh):
    rows = P(("dp", "expert"), None)
    return jax.shard_map(
        shards,
        mesh=mesh,
        in_specs=(rows, rows, rows, rows, P("expert", None, None)),
        out_specs=(rows, rows, P("expert", "dp", None)),
        check_vma=False,
    )
```

```python
import functools

import jax
import jax.numpy as jnp
from jax import lax
from jax.experimental import pallas as pl
from jax.experimental.pallas import tpu as pltpu
from jax.sharding import PartitionSpec as P

BF = jnp.bfloat16
F32 = jnp.float32
I32 = jnp.int32
D = 2048
F = 768
T = 128
CAP = 16
NZ = 8
NQ = 4
FB = 256
NF = F // FB
ROWS = NZ * NQ * CAP
EXTRA = 128
MIB = 1024 * 1024
NT = (((1,), (1,)), ((), ()))
TN = (((0,), (0,)), ((), ()))
ANY = pl.BlockSpec(memory_space=pl.ANY)
together = lax.optimization_barrier


def z_shift(value, step, mask=0):
    return lax.ppermute(value, "expert", [(i, ((i ^ mask) + NQ * step) % 32) for i in range(32)])


def plane_swap(value, mask):
    return lax.ppermute(value, "expert", [(i, i ^ mask) for i in range(32)])


def x_shift(value, step):
    return lax.ppermute(value, "dp", [(i, (i + 2 * step) % 8) for i in range(8)])


def y_swap(value):
    return lax.ppermute(value, "dp", [(i, i ^ 1) for i in range(8)])


def params(mib):
    return pltpu.CompilerParams(vmem_limit_bytes=mib * MIB)


def cost(flops, moved):
    return pl.CostEstimate(flops=flops // 1024, bytes_accessed=moved // 1024, transcendentals=0)


def columns(pairs):
    diagonal = lax.broadcasted_iota(I32, (T, T), 0) == lax.broadcasted_iota(I32, (T, T), 1)
    eye = diagonal.astype(F32).astype(BF)
    return lax.dot_general(eye, pairs.astype(F32).astype(BF), NT, preferred_element_type=F32)


def pack_kernel(tokens, cotangent, routes, probs, out, pairs, weights, meta, sems):
    loads = [
        pltpu.make_async_copy(routes, pairs, sems.at[0]),
        pltpu.make_async_copy(probs, weights, sems.at[1]),
    ]
    rows = [
        pltpu.make_async_copy(tokens, out.at[:, pl.ds(0, D)], sems.at[2]),
        pltpu.make_async_copy(cotangent, out.at[:, pl.ds(D, D)], sems.at[3]),
    ]
    for copy in loads + rows:
        copy.start()
    for copy in loads:
        copy.wait()
    lane = lax.broadcasted_iota(I32, (T, EXTRA), 1)
    r, p = columns(pairs[...]), columns(weights[...])
    value = jnp.where(lane == 0, r[:, 0:1], jnp.where(lane == 1, r[:, 1:2], 0.0))
    value += jnp.where(lane == 2, p[:, 0:1], jnp.where(lane == 3, p[:, 1:2], 0.0))
    meta[...] = value.astype(BF)
    last = pltpu.make_async_copy(meta, out.at[:, pl.ds(2 * D, EXTRA)], sems.at[4])
    last.start()
    last.wait()
    for copy in rows:
        copy.wait()


def pack(tokens, cotangent, routes, probs):
    return pl.pallas_call(
        pack_kernel,
        in_specs=[ANY] * 4,
        out_specs=ANY,
        out_shape=jax.ShapeDtypeStruct((T, 2 * D + EXTRA), BF),
        scratch_shapes=[
            pltpu.VMEM((2, T), I32),
            pltpu.VMEM((2, T), BF),
            pltpu.VMEM((T, EXTRA), BF),
            pltpu.SemaphoreType.DMA((5,)),
        ],
        cost_estimate=cost(0, 8 * T * D),
        compiler_params=params(8),
    )(tokens, cotangent, routes.T, probs.T)


def slots(r0, r1, expert, place):
    first = (r0 == expert).astype(F32)
    second = (r1 == expert).astype(F32)
    named = first + second
    row = lax.broadcasted_iota(I32, (T, T), 0)
    col = lax.broadcasted_iota(I32, (T, T), 1)
    before = (col < row).astype(F32).astype(BF)
    position = jnp.dot(before, named.astype(BF), preferred_element_type=F32)
    here = (position == place).astype(F32)
    return first * here, second * here


def select_kernel(plan, n, *refs):
    metas, ins = refs[:n], refs[n : 2 * n]
    outs, hot = refs[2 * n : -1], refs[-1]
    c = pl.program_id(0)

    @pl.when(c == 0)
    def _():
        me = lax.axis_index("expert")
        z, q = me // NQ, me % NQ
        for i, (block, step, _) in enumerate(plan):
            lane = lax.broadcasted_iota(I32, (T, NQ * CAP), 1)
            plane = (z + step + NZ) % NZ
            expert = (plane * NQ + jnp.bitwise_xor(q, lane // CAP)).astype(F32)
            place = (lane % CAP).astype(F32)
            meta = metas[block][...].astype(F32)
            one, two = slots(meta[:, 0:1], meta[:, 1:2], expert, place)
            hot[0, i] = (one + two).astype(BF)
            hot[1, i] = (one * meta[:, 2:3] + two * meta[:, 3:4]).astype(BF)

    for i, (block, _, targets) in enumerate(plan):
        rows = lax.dot_general(hot[c // 2, i], ins[block][...], TN, preferred_element_type=F32)
        rows = rows.astype(BF)
        for j, out, at in targets:
            outs[out][at : at + CAP, :] = rows[j * CAP : (j + 1) * CAP, :]


def select(plan, ins, heights):
    n = len(ins)
    width = 1024
    return pl.pallas_call(
        functools.partial(select_kernel, plan, n),
        grid=(2 * D // width,),
        in_specs=[pl.BlockSpec((T, EXTRA), lambda c: (0, 2 * D // EXTRA))] * n
        + [pl.BlockSpec((T, width), lambda c: (0, c))] * n,
        out_specs=[pl.BlockSpec((height, width), lambda c: (0, c)) for height in heights],
        out_shape=[jax.ShapeDtypeStruct((height, 2 * D), BF) for height in heights],
        scratch_shapes=[pltpu.VMEM((2, len(plan), T, NQ * CAP), BF)],
        cost_estimate=cost(2 * n * 64 * T * 2 * D, n * 3 * T * D * 2),
        compiler_params=params(12),
    )(*ins, *ins)


def dot_columns(dots):
    lane = lax.broadcasted_iota(I32, dots.shape, 1)
    high = dots.astype(BF).astype(F32)
    return jnp.where(lane == 0, high, jnp.where(lane == 1, dots - high, 0.0)).astype(BF)


def place_rows(order, out_rows, grad_all, sems):
    me = lax.axis_index("expert")
    z, q = me // NQ, me % NQ
    copies = []
    for i, (step, near) in enumerate(order):
        owner = ((z + step + NZ) % NZ) * NQ + jnp.bitwise_xor(q, near)
        copies.append(
            pltpu.make_async_copy(
                out_rows.at[pl.ds(i * CAP, CAP)],
                grad_all.at[pl.ds(pl.multiple_of(owner * CAP, CAP), CAP)],
                sems.at[i],
            )
        )
    for copy in copies:
        copy.start()
    for copy in copies:
        copy.wait()


def expert_kernel(pieces, order, grads, aliased, gate_w, up_w, down_w, *refs):
    ins = refs[: len(pieces)]
    refs = refs[len(pieces) + aliased :]
    if grads:
        xs, fac, grad_all, rows, dot_acc, acc, out_rows, sems = refs
    else:
        xs, fac, dots, rows, dot_acc = refs
    f = pl.program_id(0)

    @pl.when(f == 0)
    def _():
        at = 0
        for size, ref in zip(pieces, ins):
            rows[at : at + size, :] = ref[...]
            at += size
        dot_acc[...] = jnp.zeros_like(dot_acc)
        if grads:
            acc[...] = jnp.zeros_like(acc)

    x = rows[:, :D]
    gate = jnp.dot(x, gate_w[...], preferred_element_type=F32)
    up = jnp.dot(x, up_w[...], preferred_element_type=F32)
    dh = jnp.dot(rows[:, D:], down_w[...], preferred_element_type=F32)
    sig = jax.nn.sigmoid(gate)
    active = gate * sig
    hidden = (active * up).astype(BF)
    d_gate = (dh * up * sig * (1.0 + gate * (1.0 - sig))).astype(BF)
    d_up = (dh * active).astype(BF)
    at = pl.multiple_of(f * FB, FB)
    fac[:, pl.ds(at, FB)] = d_gate
    fac[:, pl.ds(F + at, FB)] = d_up
    fac[:, pl.ds(2 * F + at, FB)] = hidden
    prod = hidden.astype(F32) * dh
    dot_acc[...] += prod[:, :128] + prod[:, 128:]
    if grads:
        acc[...] += lax.dot_general(d_gate, gate_w[...], NT, preferred_element_type=F32)
        acc[...] += lax.dot_general(d_up, up_w[...], NT, preferred_element_type=F32)

    @pl.when(f == NF - 1)
    def _():
        dp = lax.axis_index("dp")
        xi, yi = dp // 2, dp % 2
        for part in range(2):
            for chunk in range(4):
                for half in range(2):
                    source = ((xi + chunk) % 4) * 2 + jnp.bitwise_xor(yi, half)
                    source = pl.multiple_of(part * D + source * 256, 256)
                    to = part * D + (chunk * 2 + half) * 256
                    xs[:, to : to + 256] = rows[:, pl.ds(source, 256)]
        total = jnp.sum(dot_acc[...], axis=1, keepdims=True)
        total = jnp.broadcast_to(total, dot_acc.shape)
        if grads:
            out_rows[:, :D] = acc[...].astype(BF)
            out_rows[:, D:] = dot_columns(total)
            place_rows(order, out_rows, grad_all, sems)
        else:
            dots[...] = total


def expert_pass(weights, pieces, order, block, held, grads):
    sizes = [size for _, size, _ in pieces]
    rows = sum(sizes)
    whole = lambda f: (0, 0)
    mine = lambda f: (block, 0)
    outs = [pl.BlockSpec((rows, 2 * D), mine), pl.BlockSpec((rows, 3 * F), mine)]
    shapes = [jax.ShapeDtypeStruct((ROWS, 2 * D), BF), jax.ShapeDtypeStruct((ROWS, 3 * F), BF)]
    scratch = [pltpu.VMEM((rows, 2 * D), BF), pltpu.VMEM((rows, 128), F32)]
    if grads:
        outs.append(ANY)
        shapes.append(jax.ShapeDtypeStruct((ROWS, D + EXTRA), BF))
        scratch += [
            pltpu.VMEM((rows, D), F32),
            pltpu.VMEM((rows, D + EXTRA), BF),
            pltpu.SemaphoreType.DMA((rows // CAP,)),
        ]
    else:
        outs.append(pl.BlockSpec((rows, 128), whole))
        shapes.append(jax.ShapeDtypeStruct((rows, 128), F32))
    return pl.pallas_call(
        functools.partial(expert_kernel, sizes, order, grads, len(held)),
        grid=(NF,),
        in_specs=[
            pl.BlockSpec((D, FB), lambda f: (0, f)),
            pl.BlockSpec((D, FB), lambda f: (0, f + NF)),
            pl.BlockSpec((D, FB), lambda f: (0, f + 2 * NF)),
        ]
        + [pl.BlockSpec((size, 2 * D), (lambda f, at=at: (at, 0))) for _, size, at in pieces]
        + [ANY] * len(held),
        out_specs=outs,
        out_shape=shapes,
        scratch_shapes=scratch,
        input_output_aliases={3 + len(pieces) + i: i for i in range(len(held))},
        cost_estimate=cost(2 * rows * D * (5 if grads else 3) * F, D * 3 * F * 2),
        compiler_params=params(24),
    )(weights, weights, weights, *[piece for piece, _, _ in pieces], *held)


def grad_kernel(order, gate_w, up_w, gate_f, up_f, dots, held, grad_all, acc, out_rows, sems):
    f = pl.program_id(0)

    @pl.when(f == 0)
    def _():
        acc[...] = jnp.zeros_like(acc)

    acc[...] += lax.dot_general(gate_f[...], gate_w[...], NT, preferred_element_type=F32)
    acc[...] += lax.dot_general(up_f[...], up_w[...], NT, preferred_element_type=F32)

    @pl.when(f == NF - 1)
    def _():
        out_rows[:, :D] = acc[...].astype(BF)
        out_rows[:, D:] = dot_columns(dots[...])
        place_rows(order, out_rows, grad_all, sems)


def grad_pass(weights, fac, block, dots, order, grad_all):
    rows = dots.shape[0]
    return pl.pallas_call(
        functools.partial(grad_kernel, order),
        grid=(NF,),
        in_specs=[
            pl.BlockSpec((D, FB), lambda f: (0, f)),
            pl.BlockSpec((D, FB), lambda f: (0, f + NF)),
            pl.BlockSpec((rows, FB), lambda f: (block, f)),
            pl.BlockSpec((rows, FB), lambda f: (block, f + NF)),
            pl.BlockSpec((rows, 128), lambda f: (0, 0)),
            ANY,
        ],
        out_specs=ANY,
        out_shape=jax.ShapeDtypeStruct(grad_all.shape, BF),
        scratch_shapes=[
            pltpu.VMEM((rows, D), F32),
            pltpu.VMEM((rows, D + EXTRA), BF),
            pltpu.SemaphoreType.DMA((rows // CAP,)),
        ],
        input_output_aliases={5: 0},
        cost_estimate=cost(4 * rows * D * F, D * 2 * F * 2),
        compiler_params=params(20),
    )(weights, weights, fac, fac, dots, grad_all)


def parts_kernel(counts, *refs):
    n = len(counts)
    fac = refs[n][...]
    adds, outs = refs[n + 1 : n + 1 + sum(counts)], refs[-n:]
    for i, count in enumerate(counts):
        total = lax.dot_general(refs[i][...], fac, TN, preferred_element_type=F32)
        for ref in adds[:count]:
            total += ref[...].astype(F32)
        adds = adds[count:]
        outs[i][...] = total.astype(outs[i].dtype)


def parts(xs, fac, plan, dtype, adds=None, into=None, weight=1):
    n, steps = len(plan), len(plan[0])
    adds = adds or [()] * n

    def pick(values):
        def at(f):
            index = values[-1]
            for i in range(steps - 2, -1, -1):
                index = jnp.where(f == i, values[i], index)
            return 0, index

        return at

    def side(first):
        return pl.BlockSpec((256, F), lambda f: (0, f + first))

    flat = [add for some in adds for add in some]
    held = [] if into is None or into is True else [into]
    group, total = (0, steps) if into is None else (plan[0][0][1], 3)
    return pl.pallas_call(
        functools.partial(parts_kernel, [len(some) for some in adds]),
        grid=(steps,),
        in_specs=[pl.BlockSpec((ROWS, 256), pick([b for b, _ in column])) for column in plan]
        + [pl.BlockSpec((ROWS, F), pick([g for _, g in plan[0]]))]
        + [side(first) for _, first in flat]
        + [ANY] * len(held),
        out_specs=[side(group)] * n,
        out_shape=[jax.ShapeDtypeStruct((256, F * total), dtype)] * n,
        input_output_aliases={n + 1 + len(flat): 0} if held else {},
        cost_estimate=cost(weight * 2 * n * ROWS * 256 * steps * F, 2 * ROWS * steps * F),
        compiler_params=params(16),
    )(*([xs] * n), fac, *[value for value, _ in flat], *held)


def total_kernel(n, *refs):
    value = refs[0][...].astype(F32)
    for ref in refs[1:n]:
        value += ref[...].astype(F32)
    refs[-1][...] = value.astype(refs[-1].dtype)


def total(adds, dtype, group=0, into=None):
    n = len(adds)
    held = [] if into is None or into is True else [into]
    return pl.pallas_call(
        functools.partial(total_kernel, n),
        grid=(2,),
        in_specs=[
            pl.BlockSpec((256, F // 2), lambda f, at=at: (0, 2 * at + f)) for _, at in adds
        ]
        + [ANY] * len(held),
        out_specs=pl.BlockSpec((256, F // 2), lambda f: (0, 2 * group + f)),
        out_shape=jax.ShapeDtypeStruct((256, F if into is None else 3 * F), dtype),
        input_output_aliases={n: 0} if held else {},
        cost_estimate=cost(n * 256 * F, n * 512 * F),
        compiler_params=params(8),
    )(*[value for value, _ in adds], *held)


def down_first_kernel(*refs):
    first, second, third = [refs[i][...].astype(F32) + refs[i + 3][...].astype(F32) for i in range(3)]
    to_r, to_l = refs[-2:]
    to_r[:128, :] = second[:128].astype(BF)
    to_r[128:, :] = first[128:].astype(BF)
    to_l[:128, :] = second[128:].astype(BF)
    to_l[128:, :] = third[:128].astype(BF)


def down_last_kernel(own1, own3, other1, other3, from_l, from_r, *refs):
    to_r, to_l = refs[-2:]
    first = own1[:128, :].astype(F32) + other1[:128, :].astype(F32)
    third = own3[128:, :].astype(F32) + other3[128:, :].astype(F32)
    to_r[...] = (first + from_l[:128, :].astype(F32)).astype(BF)
    to_l[...] = (third + from_r[:128, :].astype(F32)).astype(BF)


def down_sum_kernel(own, other, from_l, from_r, last_l, last_r, held, out):
    here = own[...].astype(F32) + other[...].astype(F32)
    out[:128, :] = here[:128] + from_r[128:, :].astype(F32) + last_l[...].astype(F32)
    out[128:, :] = here[128:] + from_l[128:, :].astype(F32) + last_r[...].astype(F32)


def down(kernel, ins, shapes, group=None, held=()):
    half = F // 2

    def side(rows, at):
        return pl.BlockSpec((rows, half), lambda f: (0, 2 * at + f))

    return pl.pallas_call(
        kernel,
        grid=(2,),
        in_specs=[side(value.shape[0], at) for value, at in ins] + [ANY] * len(held),
        out_specs=[side(rows, group or 0) for rows, _, _ in shapes],
        out_shape=[jax.ShapeDtypeStruct((rows, cols), dtype) for rows, cols, dtype in shapes],
        input_output_aliases={len(ins): 0} if group else {},
        cost_estimate=cost(256 * F, 512 * F),
        compiler_params=params(8),
    )(*[value for value, _ in ins], *held)


def weight_grads_of(xs, fac, finish):
    far = parts(xs, fac, [[(4, 0)], [(5, 0)]], BF)
    far_r, far_l, xs, fac = together((*far, xs, fac))
    far_r, far_l = x_shift(far_r, 1), x_shift(far_l, -1)
    near = parts(xs, fac, [[(4, 1), (3, 0), (3, 1)], [(5, 1), (6, 0), (6, 1)]], BF)
    (cross,) = parts(xs, fac, [[(9, 2), (11, 2), (13, 2), (15, 2)]], BF)
    *near, cross, fac = together((*near, cross, fac))
    near_r, near_l = together((x_shift(near[0], 1), x_shift(near[1], -1)))
    from_y = y_swap(cross)
    far_r, far_l, free = together((far_r, far_l, fac))
    homes = finish(free)
    last = parts(xs, fac, [[(2, 0)], [(7, 0)]], BF, [[(far_r, 0)], [(far_l, 0)]], None, 100000)
    lasts = [together((x_shift(last[0], 1), x_shift(last[1], -1)))]
    last = parts(
        xs, fac, [[(2, 1)], [(7, 1)]], BF, [[(near_r, 0)], [(near_l, 0)]]
    )
    lasts.append(together((x_shift(last[0], 1), x_shift(last[1], -1))))
    mine, away = parts(xs, fac, [[(0, 0), (0, 1)], [(1, 0), (1, 1)]], BF)
    (own,) = parts(xs, fac, [[(8, 2), (10, 2), (12, 2), (14, 2)]], BF)
    overs = [
        total([(away, group), (near_r, 1 + group), (lasts[group][1], 0)], BF)
        for group in range(2)
    ]
    swapped = [y_swap(over) for over in overs]
    ins = [(value, c) for value in (own, from_y) for c in (1, 2, 3)]
    to_r, to_l = down(down_first_kernel, ins, [(256, F, BF)] * 2, None, tuple(overs))
    from_l, from_r = together((x_shift(to_r, 1), x_shift(to_l, -1)))
    adds = [(mine, 0), (near_l, 1), (lasts[0][0], 0), (swapped[0], 0)]
    result = total(adds, F32, 0, True)
    ins = [(value, c) for value in (own, from_y) for c in (1, 3)]
    ins += [(from_l, 0), (from_r, 0)]
    to_r, to_l = down(down_last_kernel, ins, [(128, F, BF)] * 2)
    last_l, last_r = together((x_shift(to_r, 1), x_shift(to_l, -1)))
    last_swap, homes = together((swapped[1], homes))
    adds = [(mine, 1), (near_l, 2), (lasts[1][0], 0), (last_swap, 0)]
    result = total(adds, F32, 1, result)
    ins = [(own, 0), (from_y, 0), (from_l, 0), (from_r, 0), (last_l, 0), (last_r, 0)]
    (result,) = down(down_sum_kernel, ins, [(256, 3 * F, F32)], 2, (result,))
    return result, homes


def home_kernel(routes, probs, back, grads_out, probs_out):
    lane = lax.broadcasted_iota(I32, (T, ROWS), 1)
    expert = (lane // CAP).astype(F32)
    place = (lane % CAP).astype(F32)
    r = columns(routes[...])
    one, two = slots(r[:, 0:1], r[:, 1:2], expert, place)
    both = (one + two).astype(BF)
    grads_out[...] = jnp.dot(both, back[:, :D], preferred_element_type=F32).astype(BF)
    first = jnp.dot(one.astype(BF), back[:, D:], preferred_element_type=F32)
    second = jnp.dot(two.astype(BF), back[:, D:], preferred_element_type=F32)
    sums = [jnp.sum(first.T, axis=0, keepdims=True), jnp.sum(second.T, axis=0, keepdims=True)]
    probs_out[...] = jnp.concatenate(sums, axis=0) / probs[...].astype(F32)


def home_sums(routes, probs, back):
    return pl.pallas_call(
        home_kernel,
        out_shape=[jax.ShapeDtypeStruct((T, D), BF), jax.ShapeDtypeStruct((2, T), F32)],
        cost_estimate=cost(2 * ROWS * T * D, 2 * ROWS * D),
        compiler_params=params(16),
    )(routes.T, probs.T, back)


def shards(tokens, routes, gate_probs, cotangent, expert_weights):
    weights = expert_weights[0]

    home = pack(tokens, cotangent, routes, gate_probs)
    ahead, behind = [home], [home]
    for _ in range(2):
        ahead.append(z_shift(ahead[-1], 1))
        behind.append(z_shift(behind[-1], -1))

    def exchange(messages):
        return [messages[0]] + [plane_swap(messages[j], j) for j in range(1, NQ)]

    def order(ds):
        return [(d, j) for j in range(NQ) for d in ds]

    def each(at):
        return [(j, j, at) for j in range(NQ)]

    def whole_of(pieces, rows):
        return [(piece, rows, 0) for piece in pieces]

    sel_a = select(
        [(i, 0, each(i * CAP)) for i in range(3)], [home, ahead[1], behind[1]], [48] * NQ
    )
    got_a = exchange(sel_a)
    two_l, got_a = together((behind[2], got_a))
    plan = [
        (0, 0, each(0)),
        (1, 0, each(CAP)),
        (0, 2, [(0, 0, 32), (1, 1, 32)]),
        (1, -2, [(2, 2, 32), (3, 3, 32)]),
        (0, 1, [(j, 4, j * CAP) for j in range(NQ)]),
        (1, -1, [(j, 5, j * CAP) for j in range(NQ)]),
    ]
    *sel_b, on_r, on_l = select(plan, [ahead[2], two_l], [48] * NQ + [64] * 2)
    three_r, three_l = z_shift(on_r, 1), z_shift(on_l, -1)
    got_b = exchange(sel_b)
    held = expert_pass(weights, whole_of(got_a, 48), order((0, -1, 1)), 0, (), True)
    three_r, three_l, held = together((three_r, three_l, held))
    got_c = exchange(
        [
            jnp.concatenate([v[j * CAP : (j + 1) * CAP] for v in (three_r, three_l)], axis=0)
            for j in range(NQ)
        ]
    )
    across = [piece[2 * CAP :] for piece in got_b]
    four_r = z_shift(jnp.concatenate(across[:2], axis=0), 2)
    four_l = z_shift(jnp.concatenate(across[2:], axis=0), -2)
    held = expert_pass(weights, whole_of(got_b, 32), order((-2, 2)), 3, held, True)
    last = order((-3, 3)) + order((4,))
    pieces = whole_of(got_c + [four_r, four_l], 32)
    xs, fac, dots = expert_pass(weights, pieces, last, 1, held[:2], False)
    def finish(factors):
        rows = grad_pass(weights, factors, 1, dots, last, held[2])
        back = lax.all_to_all(
            rows.reshape(32, CAP, D + EXTRA), "expert", split_axis=0, concat_axis=0, tiled=True
        ).reshape(ROWS, D + EXTRA)
        return home_sums(routes, gate_probs, back)

    weight_grads, homes = weight_grads_of(xs, fac, finish)
    token_grads, prob_grads = homes
    return token_grads, prob_grads.T, weight_grads[None]


def solution(mesh):
    rows = P(("dp", "expert"), None)
    return jax.shard_map(
        shards,
        mesh=mesh,
        in_specs=(rows, rows, rows, rows, P("expert", None, None)),
        out_specs=(rows, rows, P("expert", "dp", None)),
        check_vma=False,
    )
```
